512 devices in a mesh: expert: 128 (over y, z, core), dp: 4 (over x).
Axes of the slice: x: 4, y: 8, z: 8, core: 2. Of those that a mesh axis runs over, the one named last changes fastest.
Arguments:
- tokens: bfloat16 [32768, 2048], P(('expert', 'dp')), may hold values from -6 to 6
- grad_out: bfloat16 [32768, 2048], P(('expert', 'dp')), may hold values from -6 to 6
- route_expert: int32 [32768, 4], P(('expert', 'dp')), may hold values from 0 to 127, all different within a row; in each aligned block of 64 rows (0 to 63, 64 to 127, ...) at most 3 rows name the same one
- route_weight: bfloat16 [32768, 4], P(('expert', 'dp')), may hold values from 0.019897461 to 0.5
- gate_up_weight: bfloat16 [128, 2048, 768], P('expert', 'dp'), may hold values from -0.125 to 0.125
- down_weight: bfloat16 [128, 2048, 384], P('expert', 'dp'), may hold values from -0.3125 to 0.3125
Outputs:
- grad_tokens: bfloat16 [32768, 2048], P(('expert', 'dp'))
- grad_route: bfloat16 [32768, 4], P(('expert', 'dp'))
- grad_gate_up: float32 [128, 2048, 768], P('expert', 'dp')
- grad_down: float32 [128, 2048, 384], P('expert', 'dp')
The draws below stay inside these ranges and needn't reach their ends.
Inputs may be any that keep to these rules, and one draw needn't show every extreme that they name: `route_expert`: each row names 4 different experts. In the 64 rows of one device (aligned blocks) no expert is named by more than 3 rows, a bound that some block reaches.
All inputs are finite; a program needn't handle non-finite values.
Results may differ from the reference program's by a relative error of at most 0.01.
Values may be sent and summed in bfloat16 or wider, within the bound.
A program may use at most 64 MiB of HBM per device.

```python
import math
import jax
import jax.numpy as jnp
import numpy as np
from jax import lax

D = 2048
F = 384
TOP = 4
TOK_DEV = 64
EXPERTS = 128
CAP = 3
TOKENS = 32768
N_EXPERT = 128
N_DP = 4


def block_scale(stream_key, dims, cuts, low, high):
    level, own = 1.0, jax.random.fold_in(stream_key, 6)
    for axis_at, shards_of in cuts:
        draws = jnp.exp(jax.random.uniform(jax.random.fold_in(own, axis_at), (shards_of,), jnp.float32, low / len(cuts), high / len(cuts)))
        level = level * jnp.repeat(draws, dims[axis_at] // shards_of).reshape([-1 if axis == axis_at else 1 for axis in range(len(dims))])
    return level


def shared_out(own_key, own, number, rows, number_of, top, limit, slope):
    ranking = jax.random.permutation(own_key, number_of)
    packed, ordinary = shares(number_of, rows * top, limit, slope, True), shares(number_of, rows * top, limit, slope, False)
    places = jnp.arange(number_of)

    def named(tallies, turn):
        used = int((tallies > 0).sum())
        fixed = max(1, used // 4)
        moved = fixed + (places - fixed + turn * (used - fixed)) % max(1, number_of - fixed)
        return jnp.zeros((number_of,), jnp.int32).at[ranking[jnp.where(places < fixed, places, moved)]].set(jnp.asarray(tallies, jnp.int32))

    tallies = jnp.where(number % 4 == 0, named(packed, number // 4), named(ordinary, number - number // 4 - 1))
    mixed = jax.random.permutation(jax.random.fold_in(own, 3), number_of)
    giver, sink = mixed[0:number_of // 2 * 2:2], mixed[1:number_of // 2 * 2:2]
    room = jnp.minimum(tallies[giver] - 1, limit - tallies[sink]) // 2
    room = jnp.where((giver == ranking[0]) | (sink == ranking[0]) | (tallies[sink] == 0), 0, jnp.maximum(room, 0))
    moved = jax.random.randint(jax.random.fold_in(own, 4), (number_of // 2,), 0, 1 << 20) % (room + 1)
    tallies = tallies.at[giver].add(-moved).at[sink].add(moved)
    members = jnp.searchsorted(jnp.cumsum(tallies), jnp.arange(rows * top), side="right").astype(jnp.int32)
    listing = members.reshape(top, rows).T
    listing = listing[jax.random.permutation(jax.random.fold_in(own, 1), rows)]
    turn = jax.random.randint(jax.random.fold_in(own, 2), (rows, 1), 0, top)
    return jnp.take_along_axis(listing, (jnp.arange(top)[None, :] + turn) % top, axis=1)


def shares(number_of, total, most, lean, full):
    weights = [(1 << 20) // math.isqrt(standing ** lean) + 1 for standing in range(1, number_of + 1)]
    largest = most if full else min(most, max(-(-total // number_of), total * weights[0] // sum(weights)))
    least = 1 if total - largest >= number_of - 1 else 0
    given, spare = [largest] + [least] * (number_of - 1), total - largest - least * (number_of - 1)
    while spare > 0:
        free = [i for i in range(1, number_of) if given[i] < largest] or [i for i in range(1, number_of) if given[i] < most]
        pool, left = sum([weights[i] for i in free]), spare
        for i in free:
            more = min(most - given[i], max(1, left * weights[i] // pool), spare)
            given[i] = given[i] + more
            spare = spare - more
    return np.array(given)


def noise(stream_key, shape, spread, limit, split=(), kind=jnp.bfloat16):
    array = jax.random.normal(stream_key, shape, jnp.float32) * spread
    if len(split) > 0:
        array = block_scale(stream_key, shape, split, -0.22, 0.18) * array
    return jnp.clip(array, min=-limit, max=limit).astype(kind)


def setup_inputs(seed: int = 0) -> dict:
    keys = jax.random.split(jax.random.key(seed), 7)
    tokens = noise(keys[0], (TOKENS, D), 1.0, 6.0, ((0, 512),))
    grad_out = noise(keys[1], (TOKENS, D), 1.0, 6.0, ((0, 512),))
    route_expert_keys = jax.random.split(jax.random.fold_in(keys[2], 1), TOKENS // TOK_DEV)
    route_expert_turns = jax.random.permutation(jax.random.fold_in(keys[2], 3), TOKENS // TOK_DEV)
    route_expert = jax.vmap(lambda own, number: shared_out(jax.random.fold_in(keys[2], 2), own, number, TOK_DEV, EXPERTS, TOP, CAP, 2))(route_expert_keys, route_expert_turns).reshape((TOKENS, TOP))
    route_weight = jnp.clip(jnp.exp(math.log(0.5) - 3.224016 * jax.random.uniform(keys[3], (TOKENS, TOP), jnp.float32) ** block_scale(keys[3], (TOKENS, TOP), ((0, 512),), -0.2, 0.2)), 0.019897461, 0.5).astype(jnp.bfloat16)
    gate_up_weight = noise(keys[4], (EXPERTS, D, 2 * F), D ** -0.5, 0.125, ((0, 128), (1, 4)))
    down_weight = noise(keys[5], (EXPERTS, D, F), F ** -0.5, 0.3125, ((0, 128), (1, 4)))
    return dict(tokens=tokens, grad_out=grad_out, route_expert=route_expert, route_weight=route_weight, gate_up_weight=gate_up_weight, down_weight=down_weight)


def rounded(value):
    return lax.optimization_barrier(value.astype(jnp.bfloat16)).astype(jnp.float32)


def swish(value):
    return value * jax.nn.sigmoid(value)


def reference(tokens, grad_out, route_expert, route_weight, gate_up_weight, down_weight):
    total_rows = tokens.shape[0]
    flat_expert = route_expert.reshape(-1)
    flat_weight = route_weight.reshape(-1).astype(jnp.float32)
    pair_total = flat_expert.shape[0]
    slot_total = CAP * N_EXPERT * N_DP
    high = lax.Precision.HIGHEST

    def per_expert(carry, expert):
        grad_acc, route_acc = carry
        chosen = flat_expert == expert
        position = jnp.cumsum(chosen.astype(jnp.int32)) - 1
        target = jnp.where(chosen, position, slot_total).astype(jnp.int32)
        source = jnp.zeros((slot_total,), jnp.int32).at[target].set(jnp.arange(pair_total, dtype=jnp.int32), mode="drop")
        filled = jnp.zeros((slot_total,), jnp.float32).at[target].set(1.0, mode="drop")
        token_row = source // TOP
        rows_x = tokens[token_row].astype(jnp.float32) * filled[:, None]
        rows_dy = grad_out[token_row].astype(jnp.float32) * filled[:, None]
        rows_w = flat_weight[source] * filled
        in_mat = lax.dynamic_index_in_dim(gate_up_weight, expert, 0, keepdims=False).astype(jnp.float32)
        out_mat = lax.dynamic_index_in_dim(down_weight, expert, 0, keepdims=False).astype(jnp.float32)
        pre = jnp.dot(rows_x, in_mat, precision=high, preferred_element_type=jnp.float32)
        gate_pre = pre[:, :F]
        up_pre = pre[:, F:]
        act = swish(gate_pre)
        hidden = rounded(act * up_pre)
        expert_out = jnp.dot(hidden, out_mat.T, precision=high, preferred_element_type=jnp.float32)
        route_grad = rounded(jnp.sum(rows_dy * expert_out, axis=1))
        scaled = rounded(rows_w[:, None] * rows_dy)
        grad_hidden = jnp.dot(scaled, out_mat, precision=high, preferred_element_type=jnp.float32)
        sig = jax.nn.sigmoid(gate_pre)
        grad_gate = grad_hidden * up_pre * sig * (1.0 + gate_pre * (1.0 - sig))
        grad_up = grad_hidden * act
        grad_pre = rounded(jnp.concatenate([grad_gate, grad_up], axis=1))
        rows_grad = rounded(jnp.dot(grad_pre, in_mat.T, precision=high, preferred_element_type=jnp.float32))
        grad_in = jnp.dot(rows_x.T, grad_pre, precision=high, preferred_element_type=jnp.float32)
        grad_outw = jnp.dot(scaled.T, hidden, precision=high, preferred_element_type=jnp.float32)
        live = filled > 0
        grad_acc = grad_acc.at[jnp.where(live, token_row, total_rows).astype(jnp.int32)].add(rows_grad, mode="drop")
        route_acc = route_acc.at[jnp.where(live, source, pair_total).astype(jnp.int32)].set(route_grad, mode="drop")
        return (grad_acc, route_acc), (grad_in, grad_outw)

    start = (jnp.zeros((total_rows, D), jnp.float32), jnp.zeros((pair_total,), jnp.float32))
    (grad_acc, route_acc), (grad_gate_up, grad_down) = lax.scan(per_expert, start, jnp.arange(EXPERTS, dtype=jnp.int32))
    grad_tokens = grad_acc.astype(jnp.bfloat16)
    grad_route = route_acc.reshape(total_rows, TOP).astype(jnp.bfloat16)
    return (grad_tokens, grad_route, grad_gate_up, grad_down)
```

```python
import functools
import math

import jax
import jax.numpy as jnp
import numpy as np
from jax import lax
from jax.experimental import pallas as pl
from jax.experimental.pallas import tpu as pltpu
from jax.sharding import PartitionSpec as P

BF = jnp.bfloat16
F32 = jnp.float32
LANES = 128


def dot(a, b, dims=((1,), (0,))):
    return lax.dot_general(a, b, (dims, ((), ())), preferred_element_type=F32)


def kernel(n, cap, dpn, x_ref, dy_ref, info_ref, perm_ref, wgu_ref, wdn_ref,
           gt_ref, gr_ref, dgu_ref, ddn_ref,
           buf, infob, infor, sel, sb, xs, wgu, wdn, pre_s, gp_s, hid_s, ret, back,
           rs_out, rs_in, fin, finr, d0, d1, r0, r1,
           p0_s, p0_r, ag_s, ag_r, a2_s, a2_r, w_s, w_r, bk_s, bk_r, rs_s, rs_r, f_s, f_r,
           dp_s, dp_r):
    half_n = n // 2
    ch = 2 * n * cap
    tok, width = x_ref.shape
    wh = width // 2
    hid = wdn_ref.shape[1]
    blk = wgu_ref.shape[0]
    e = lax.axis_index("expert")
    d = lax.axis_index("dp")
    c = lax.rem(e, 2)
    z = lax.rem(e // 2, n)
    y = e // (2 * n)
    first = c == 0
    p = jnp.where(first, y, z)
    bm = jnp.where(first, z, y)

    def dev(yy, zz, cc):
        return {"expert": (yy * n + zz) * 2 + cc}

    def ring(k):
        at = lax.rem(p + k + n, n)
        return {"expert": jnp.where(first, (at * n + z) * 2, (y * n + at) * 2 + 1)}

    def other(b, cc):
        return {"expert": jnp.where(first, (y * n + b) * 2 + cc, (b * n + z) * 2 + cc)}

    sib = dev(y, z, 1 - c)
    right, left = lax.rem(d + 1, dpn), lax.rem(d + dpn - 1, dpn)

    def remote(src, dst, ss, rs, to):
        return pltpu.make_async_remote_copy(
            src_ref=src, dst_ref=dst, send_sem=ss, recv_sem=rs, device_id=to,
            device_id_type=pl.DeviceIdType.MESH)

    barrier = pltpu.get_barrier_semaphore()

    def greet(to):
        pl.semaphore_signal(barrier, inc=1, device_id=to, device_id_type=pl.DeviceIdType.MESH)

    @pl.loop(0, n)
    def _(b):
        for cc in range(2):
            @pl.when(jnp.logical_not(jnp.logical_and(b == z, c == cc)))
            def _():
                greet(dev(y, b, cc))

            @pl.when(b != y)
            def _():
                greet(dev(b, z, cc))

    if dpn > 1:
        greet({"dp": right})
        greet({"dp": left})
    pl.semaphore_wait(barrier, 4 * n - 3 + (2 if dpn > 1 else 0))

    pending = []

    def go(copy):
        copy.start()
        pending.append(copy)
        return copy

    psib = jnp.where(first, z, y)
    mine = pl.ds(pl.multiple_of(c * tok, tok), tok)
    mycol = pl.ds(pl.multiple_of(c * wh, wh), wh)
    hiscol = pl.ds(pl.multiple_of((1 - c) * wh, wh), wh)
    swap = [
        go(remote(info_ref.at[1 - c], infor, p0_s.at[2], p0_r.at[2], sib)),
        go(remote(x_ref.at[:, hiscol], buf.at[0, psib, mine], p0_s.at[0], p0_r.at[0], sib)),
        go(remote(dy_ref.at[:, hiscol], buf.at[1, psib, mine], p0_s.at[1], p0_r.at[1], sib)),
    ]

    if dpn > 1:
        wcopies = []
        for k, (src, dst) in enumerate(((wgu_ref, wgu), (wdn_ref, wdn))):
            wcopies.append(go(remote(src, dst.at[d], w_s.at[0, 0, k], w_r.at[0, 0, k], {"dp": right})))
            wcopies.append(go(remote(src, dst.at[d], w_s.at[0, 1, k], w_r.at[0, 1, k], {"dp": left})))

    buf[0, p, mine] = x_ref[:, mycol]
    buf[1, p, mine] = dy_ref[:, mycol]
    wgu[d] = wgu_ref[...]
    wdn[d] = wdn_ref[...]

    def ag(s, way, a):
        at = lax.rem(p - s + n, n) if way == 0 else lax.rem(p + s, n)
        if a == 2:
            ref = infob.at[at]
        elif s == half_n - 1:
            ref = buf.at[a, at, pl.ds(way * tok, tok)]
        else:
            ref = buf.at[a, at]
        return remote(ref, ref, ag_s.at[way, s, a], ag_r.at[way, s, a], ring(1 if way == 0 else -1))

    def ag_runs(s, way, a):
        return not (a == 2 and s == half_n - 1 and way == 1)

    swap[0].wait_recv()
    infob[p] = info_ref[c] + infor[...]
    copies = {}
    for a in (2, 0, 1):
        if a < 2:
            swap[a + 1].wait_recv()
        for way in range(2):
            if ag_runs(0, way, a):
                copies[0, way, a] = go(ag(0, way, a))
    for s in range(1, half_n):
        for a in (2, 0, 1):
            for way in range(2):
                copies[s - 1, way, a].wait_recv()
            for way in range(2):
                if ag_runs(s, way, a):
                    copies[s, way, a] = go(ag(s, way, a))
    copies[half_n - 1, 0, 2].wait_recv()

    base = (p * (n * 2 * ch) + 1).astype(F32)
    lanes = 2 * tok

    @pl.loop(0, n)
    def _(at):
        block = infob[at]
        rows = lax.broadcasted_iota(jnp.int32, (2 * n * ch, lanes), 0).astype(F32)
        picked = jnp.zeros((2 * n * ch, lanes), F32)
        scaled = jnp.zeros((2 * n * ch, lanes), F32)
        for k in range(4):
            hit = rows == (block[k:k + 1, :] - base)
            picked = jnp.where(hit, 1.0, picked)
            scaled = jnp.where(hit, block[4 + k:5 + k, :], scaled)
        cols = pl.ds(pl.multiple_of(at * lanes, lanes), lanes)
        sel[0, :, cols] = picked.astype(BF)
        sel[1, :, cols] = scaled.astype(BF)

    def dispatch(a):
        for way in range(2):
            copies[half_n - 1, way, a].wait_recv()

        @pl.loop(0, half_n)
        def _(g):
            places = (lax.rem(bm + g, n), lax.rem(bm + g + half_n, n))
            spans = [pl.ds(pl.multiple_of(b * (2 * ch), 2 * ch), 2 * ch) for b in places]
            lhs = jnp.concatenate([sel[a, span, :] for span in spans], axis=0)
            rows = dot(lhs, buf[a].reshape(n * lanes, wh)).astype(BF)
            for i, (b, span) in enumerate(zip(places, spans)):
                sb[a, span, :] = rows[i * 2 * ch:(i + 1) * 2 * ch]
                for cc in range(2):
                    src = sb.at[a, pl.ds(pl.multiple_of((b * 2 + cc) * ch, ch), ch)]
                    dst = xs.at[a, c, pl.ds(pl.multiple_of(bm * ch, ch), ch)]
                    own = jnp.logical_and(b == bm, c == cc)

                    @pl.when(own)
                    def _():
                        pltpu.make_async_copy(src, dst, a2_r.at[a, c, bm]).start()

                    @pl.when(jnp.logical_not(own))
                    def _():
                        remote(src, dst, a2_s.at[a, b * 2 + cc], a2_r.at[a, c, bm], other(b, cc)).start()

    def arrived(a):
        @pl.loop(0, n)
        def _(b):
            for h in range(2):
                ref = xs.at[a, h, pl.ds(pl.multiple_of(b * ch, ch), ch)]
                pltpu.make_async_copy(ref, ref, a2_r.at[a, h, b]).wait()

        xs[a, 1] = dot(perm_ref[...], xs[a, 1]).astype(BF)

    dispatch(0)
    dispatch(1)

    if dpn > 1:
        halfb = blk // 2
        for copy in wcopies:
            copy.wait_recv()
        wc2 = []
        for k, dst in enumerate((wgu, wdn)):
            top, low = dst.at[left, pl.ds(0, halfb)], dst.at[right, pl.ds(halfb, halfb)]
            wc2.append(go(remote(top, top, w_s.at[1, 0, k], w_r.at[1, 0, k], {"dp": right})))
            wc2.append(go(remote(low, low, w_s.at[1, 1, k], w_r.at[1, 1, k], {"dp": left})))

    def part(t):
        per = wh // blk
        return t // per, pl.ds(pl.multiple_of(lax.rem(t, per) * blk, blk), blk)

    arrived(0)
    if dpn > 1:
        for copy in wc2:
            copy.wait_recv()
    wgu_h = [wgu[h * dpn // 2:(h + 1) * dpn // 2].reshape(wh, 2 * hid) if dpn > 1
             else wgu[0, h * wh:(h + 1) * wh] for h in range(2)]
    wdn_h = [wdn[h * dpn // 2:(h + 1) * dpn // 2].reshape(wh, hid) if dpn > 1
             else wdn[0, h * wh:(h + 1) * wh] for h in range(2)]
    pre_s[...] = dot(xs[0, 0], wgu_h[0]) + dot(xs[0, 1], wgu_h[1])
    arrived(1)
    gh = dot(xs[1, 0], wdn_h[0]) + dot(xs[1, 1], wdn_h[1])
    gate, up = pre_s[:, :hid], pre_s[:, hid:]
    sig = jax.nn.sigmoid(gate)
    act = gate * sig
    hidden = (act * up).astype(BF)
    hid_s[...] = hidden
    gp_s[:, :hid] = (gh * up * sig * (1.0 + gate * (1.0 - sig))).astype(BF)
    gp_s[:, hid:] = (gh * act).astype(BF)
    weight_grad = jnp.sum(hidden.astype(F32) * gh, axis=1, keepdims=True)
    coarse = weight_grad.astype(BF).astype(F32)
    lane = lax.broadcasted_iota(jnp.int32, (n * ch, LANES), 1)
    spot = lane == lax.rem(e, LANES)
    ret[0, :, wh:] = jnp.where(spot, coarse, 0.0).astype(BF)
    fine = jnp.where(spot, weight_grad - coarse, 0.0).astype(BF)
    ret[1, :, wh:] = dot(perm_ref[...], fine).astype(BF)
    for h in range(2):
        rows = dot(gp_s[...], wgu_h[h], ((1,), (1,))).astype(BF)
        if h == 1:
            rows = dot(perm_ref[...], rows).astype(BF)
        ret[h, :, :wh] = rows

        @pl.loop(0, n)
        def _(i):
            b = lax.rem(bm + i, n)
            src = ret.at[h, pl.ds(pl.multiple_of(b * ch, ch), ch)]
            q = (z if h == 0 else y) * 2 + c
            dst = back.at[pl.ds(pl.multiple_of(q * ch, ch), ch)]
            own = jnp.logical_and(c == h, b == bm)

            @pl.when(own)
            def _():
                pltpu.make_async_copy(src, dst, bk_r.at[q]).start()

            @pl.when(jnp.logical_not(own))
            def _():
                to = dev(y, b, 0) if h == 0 else dev(b, z, 1)
                remote(src, dst, bk_s.at[h, b], bk_r.at[q], to).start()

    def weight_part(t):
        h, cols = part(t)
        return (dot(xs[0, h, :, cols], gp_s[...], ((0,), (0,))),
                dot(xs[1, h, :, cols], hid_s[...], ((0,), (0,))))

    if dpn > 1:
        both = ((0, {"dp": right}, 0), (1, {"dp": left}, halfb))
        far = weight_part(lax.rem(d + 2, dpn))
        d0[:, :2 * hid] = far[0].astype(BF)
        d0[:, 2 * hid:] = far[1].astype(BF)
        far_copies = [go(remote(d0.at[pl.ds(off, halfb)], r0.at[way], dp_s.at[0, way], dp_r.at[0, way], to))
                      for way, to, off in both]
    own_gu, own_dn = weight_part(d)
    dgu_ref[...] = own_gu
    ddn_ref[...] = own_dn

    @pl.loop(0, 2 * n)
    def _(q):
        ref = back.at[pl.ds(pl.multiple_of(q * ch, ch), ch)]
        pltpu.make_async_copy(ref, ref, bk_r.at[q]).wait()

    def share(t):
        cols = pl.ds(pl.multiple_of(t * lanes, lanes), lanes)
        return dot(sel[0, :, cols], back[...], ((0,), (0,)))

    def rs(s, way):
        rows = pl.ds(way * tok, tok) if s == 0 else pl.ds(0, lanes)
        return remote(rs_out.at[way, s, rows], rs_in.at[way, s, rows],
                      rs_s.at[way, s], rs_r.at[way, s], ring(1 if way == 0 else -1))

    whole = share(lax.rem(p + half_n, n)).astype(BF)
    rcopies = {}
    for way in range(2):
        rs_out[way, 0] = whole
        rcopies[0, way] = go(rs(0, way))

    def dp_second():
        out = []
        for way, to, off in both:
            gu, dn = weight_part(right if way == 0 else left)
            far_copies[way].wait_recv()
            d1[way, :, :2 * hid] = gu.astype(BF)
            d1[way, :, 2 * hid:] = dn.astype(BF)
            got = r0[way].astype(F32)
            here = slice(off, off + halfb)
            d1[way, here, :2 * hid] = (gu[here] + got[:, :2 * hid]).astype(BF)
            d1[way, here, 2 * hid:] = (dn[here] + got[:, 2 * hid:]).astype(BF)
            out.append(go(remote(d1.at[way], r1.at[way], dp_s.at[1, way], dp_r.at[1, way], to)))
        return out

    if dpn > 1:
        near = dp_second()
    for s in range(1, half_n):
        for way in range(2):
            mine_part = share(lax.rem(p + half_n - s if way == 0 else p + half_n + s, n))
            rcopies[s - 1, way].wait_recv()
            if s == 1:
                there = slice(way * tok, way * tok + tok)
                rs_out[way, s] = mine_part.astype(BF)
                rs_out[way, s, there] = (mine_part[there] + rs_in[way, 0, there].astype(F32)).astype(BF)
            else:
                rs_out[way, s] = (mine_part + rs_in[way, s - 1].astype(F32)).astype(BF)
            rcopies[s, way] = go(rs(s, way))
    total = share(p)
    last = half_n - 1
    for way in range(2):
        rcopies[last, way].wait_recv()
    if half_n == 1:
        for way in range(2):
            there = slice(way * tok, way * tok + tok)
            fin[there] = (total[there] + rs_in[way, 0, there].astype(F32)).astype(BF)
    else:
        fin[...] = (total + rs_in[0, last].astype(F32) + rs_in[1, last].astype(F32)).astype(BF)
    his = pl.ds(pl.multiple_of((1 - c) * tok, tok), tok)
    swapped = go(remote(fin.at[his], finr, f_s, f_r, sib))
    gt_ref[:, mycol] = fin[mine, :wh]
    swapped.wait_recv()
    gt_ref[:, hiscol] = finr[:, :wh]
    gr_ref[...] = fin[mine, wh:].astype(F32) + finr[:, wh:].astype(F32)

    if dpn > 1:
        for copy in near:
            copy.wait_recv()
        dgu_ref[...] += r1[0, :, :2 * hid].astype(F32) + r1[1, :, :2 * hid].astype(F32)
        ddn_ref[...] += r1[0, :, 2 * hid:].astype(F32) + r1[1, :, 2 * hid:].astype(F32)

    for copy in pending:
        copy.wait_send()

    @pl.loop(0, n)
    def _(b):
        for a in range(2):
            for cc in range(2):
                @pl.when(jnp.logical_not(jnp.logical_and(b == bm, c == cc)))
                def _():
                    ref = sb.at[a, pl.ds(pl.multiple_of((b * 2 + cc) * ch, ch), ch)]
                    pltpu.make_async_copy(ref, ref, a2_s.at[a, b * 2 + cc]).wait()
        for h in range(2):
            @pl.when(jnp.logical_not(jnp.logical_and(c == h, b == bm)))
            def _():
                ref = ret.at[h, pl.ds(pl.multiple_of(b * ch, ch), ch)]
                pltpu.make_async_copy(ref, ref, bk_s.at[h, b]).wait()


def on_device(n, dpn, tokens, grad_out, route_expert, route_weight, gate_up_weight, down_weight):
    tok, width = tokens.shape
    top = route_expert.shape[1]
    wh = width // 2
    blk, hid = down_weight.shape[1:]
    experts = 2 * n * n
    cap = min(tok, (tok * top + experts - 1) // experts + 1)
    ch = 2 * n * cap
    lanes = 2 * tok
    me = lax.axis_index("expert")
    c, z, y = me % 2, (me // 2) % n, me // (2 * n)

    chosen = route_expert.T
    flat = chosen.reshape(-1)
    owner = jnp.arange(top * tok, dtype=jnp.int32) % tok
    earlier = (flat[:, None] == flat[None, :]) & (owner[None, :] < owner[:, None])
    rank = jnp.sum(earlier.astype(jnp.int32), axis=1).reshape(top, tok)
    ec, ez, ey = chosen % 2, (chosen // 2) % n, chosen // (2 * n)
    by_y = ((ey * (2 * n) + ez * 2 + ec) * ch) + rank * (2 * n) + y * 2 + c + 1
    by_z = ((ez * (2 * n) + ey * 2 + ec) * ch) + rank * (2 * n) + z * 2 + c + 1
    weight = route_weight.T.astype(F32)
    info = jnp.stack([jnp.concatenate([code.astype(F32), weight], axis=0) for code in (by_y, by_z)])
    info = jnp.concatenate([jnp.where(c == 0, info, 0.0), jnp.where(c == 1, info, 0.0)], axis=2)

    at = np.arange(n * ch)
    hop = (at % (2 * n)) // 2 * ch + (at % ch) // (2 * n) * (2 * n) + at // ch * 2 + at % 2
    perm = np.zeros((n * ch, n * ch), np.float32)
    perm[at, hop] = 1.0
    perm = jnp.asarray(perm, BF)

    vm = pl.BlockSpec(memory_space=pltpu.VMEM)
    half_n = n // 2
    dma = pltpu.SemaphoreType.DMA
    all_rows = 2 * n * ch
    wx = wh + LANES
    cut = 3 * hid
    scratch = [
        pltpu.VMEM((2, n, lanes, wh), BF),
        pltpu.VMEM((n, 8, lanes), F32),
        pltpu.VMEM((8, lanes), F32),
        pltpu.VMEM((2, all_rows, n * lanes), BF),
        pltpu.VMEM((2, all_rows, wh), BF),
        pltpu.VMEM((2, 2, n * ch, wh), BF),
        pltpu.VMEM((dpn, blk, 2 * hid), BF),
        pltpu.VMEM((dpn, blk, hid), BF),
        pltpu.VMEM((n * ch, 2 * hid), F32),
        pltpu.VMEM((n * ch, 2 * hid), BF),
        pltpu.VMEM((n * ch, hid), BF),
        pltpu.VMEM((2, n * ch, wx), BF),
        pltpu.VMEM((all_rows, wx), BF),
        pltpu.VMEM((2, half_n, lanes, wx), BF),
        pltpu.VMEM((2, half_n, lanes, wx), BF),
        pltpu.VMEM((lanes, wx), BF),
        pltpu.VMEM((tok, wx), BF),
        pltpu.VMEM((blk, cut), BF),
        pltpu.VMEM((2, blk, cut), BF),
        pltpu.VMEM((2, blk // 2, cut), BF),
        pltpu.VMEM((2, blk, cut), BF),
        dma((3,)), dma((3,)),
        dma((2, half_n, 3)), dma((2, half_n, 3)),
        dma((2, 2 * n)), dma((2, 2, n)),
        dma((2, 2, 2)), dma((2, 2, 2)),
        dma((2, n)), dma((2 * n,)),
        dma((2, half_n)), dma((2, half_n)),
        dma, dma,
        dma((2, 2)), dma((2, 2)),
    ]
    grad_tokens, grad_w, grad_gu, grad_dn = pl.pallas_call(
        functools.partial(kernel, n, cap, dpn),
        out_shape=(
            jax.ShapeDtypeStruct((tok, width), BF),
            jax.ShapeDtypeStruct((tok, LANES), F32),
            jax.ShapeDtypeStruct((blk, 2 * hid), F32),
            jax.ShapeDtypeStruct((blk, hid), F32),
        ),
        in_specs=[vm] * 6,
        out_specs=(vm, vm, vm, vm),
        scratch_shapes=scratch,
        compiler_params=pltpu.CompilerParams(
            collective_id=0, has_side_effects=True, vmem_limit_bytes=60 * 1024 * 1024),
    )(tokens, grad_out, info, perm, gate_up_weight[0], down_weight[0])
    picked = route_expert[:, :, None] == jnp.arange(LANES, dtype=jnp.int32)[None, None, :]
    grad_route = jnp.sum(jnp.where(picked, grad_w[:, None, :], 0.0), axis=2)
    grad_route = (grad_route / route_weight.astype(F32)).astype(BF)
    return grad_tokens, grad_route, grad_gu[None], grad_dn[None]


def solution(mesh):
    n = math.isqrt(mesh.shape["expert"] // 2)
    return jax.shard_map(
        functools.partial(on_device, n, mesh.shape["dp"]),
        mesh=mesh,
        in_specs=(
            P(("expert", "dp"), None),
            P(("expert", "dp"), None),
            P(("expert", "dp"), None),
            P(("expert", "dp"), None),
            P("expert", "dp", None),
            P("expert", "dp", None),
        ),
        out_specs=(
            P(("expert", "dp"), None),
            P(("expert", "dp"), None),
            P("expert", "dp", None),
            P("expert", "dp", None),
        ),
        check_vma=False,
    )
```

```python
import functools
import math

import jax
import jax.numpy as jnp
import numpy as np
from jax import lax
from jax.experimental import pallas as pl
from jax.experimental.pallas import tpu as pltpu
from jax.sharding import PartitionSpec as P

BF = jnp.bfloat16
F32 = jnp.float32
LANES = 128


def dot(a, b, dims=((1,), (0,))):
    return lax.dot_general(a, b, (dims, ((), ())), preferred_element_type=F32)


def kernel(n, cap, dpn, x_ref, dy_ref, route_ref, weight_ref, perm_ref, wgu_ref, wdn_ref,
           gt_ref, gr_ref, dgu_ref, ddn_ref,
           buf, info, infob, infor, sel, sb, xs, wgu, wdn, pre_s, gp_s, hid_s, ret, back,
           rs_out, rs_in, fin, finr, d0, d1, r0, r1, xa, gpa, g_out, g_in, g_col, g_part, g_all, g_fin,
           p0_s, p0_r, ag_s, ag_r, in_s, in_r, a2_s, a2_r, w_s, w_r, bk_s, bk_r, rs_s, rs_r,
           f_s, f_r, dp_s, dp_r, gb_s, gb_r, gs_s, gs_r, gf_s, gf_r, xb_s, xb_r, gp_sem_s, gp_sem_r):
    half_n = n // 2
    ch = 2 * n * cap
    tok, width = x_ref.shape
    wh = width // 2
    hid = wdn_ref.shape[1]
    blk = wgu_ref.shape[0]
    e = lax.axis_index("expert")
    d = lax.axis_index("dp")
    c = lax.rem(e, 2)
    z = lax.rem(e // 2, n)
    y = e // (2 * n)
    first = c == 0
    p = jnp.where(first, y, z)
    bm = jnp.where(first, z, y)

    def dev(yy, zz, cc):
        return {"expert": (yy * n + zz) * 2 + cc}

    def ring(k):
        at = lax.rem(p + k + n, n)
        return {"expert": jnp.where(first, (at * n + z) * 2, (y * n + at) * 2 + 1)}

    def other(b, cc):
        return {"expert": jnp.where(first, (y * n + b) * 2 + cc, (b * n + z) * 2 + cc)}

    sib = dev(y, z, 1 - c)
    right, left = lax.rem(d + 1, dpn), lax.rem(d + dpn - 1, dpn)

    def remote(src, dst, ss, rs, to):
        return pltpu.make_async_remote_copy(
            src_ref=src, dst_ref=dst, send_sem=ss, recv_sem=rs, device_id=to,
            device_id_type=pl.DeviceIdType.MESH)

    barrier = pltpu.get_barrier_semaphore()

    def greet(to):
        pl.semaphore_signal(barrier, inc=1, device_id=to, device_id_type=pl.DeviceIdType.MESH)

    @pl.loop(0, n)
    def _(b):
        for cc in range(2):
            @pl.when(jnp.logical_not(jnp.logical_and(b == z, c == cc)))
            def _():
                greet(dev(y, b, cc))

            @pl.when(b != y)
            def _():
                greet(dev(b, z, cc))

    greet({"dp": right})
    greet({"dp": left})

    experts = 2 * n * n
    lanes = 2 * tok
    base = (p * (n * 2 * ch) + 1).astype(F32)
    spot = lax.broadcasted_iota(jnp.int32, (tok, lanes), 1) - lax.broadcasted_iota(jnp.int32, (tok, lanes), 0)
    spread = jnp.where(spot == c * tok, 1.0, 0.0).astype(BF)
    lane = lax.broadcasted_iota(jnp.int32, (1, lanes), 1)
    held = jnp.logical_and(lane >= c * tok, lane < c * tok + tok)
    routes = dot(route_ref[...].astype(F32).astype(BF), spread)
    gates = dot(weight_ref[...], spread)
    routes = jnp.where(held, routes, -1.0)
    expert_row = lax.broadcasted_iota(jnp.int32, (experts, lanes), 0).astype(F32)
    hits = [routes[k:k + 1] == expert_row for k in range(4)]
    named = jnp.zeros((experts, lanes), F32)
    for hit in hits:
        named = jnp.where(hit, 1.0, named)
    earlier = (lax.broadcasted_iota(jnp.int32, (lanes, lanes), 0)
               < lax.broadcasted_iota(jnp.int32, (lanes, lanes), 1))
    before = dot(named.astype(BF), jnp.where(earlier, 1.0, 0.0).astype(BF))
    level = lax.broadcasted_iota(jnp.int32, (8, lanes), 0)
    picks = [jnp.zeros((8, lanes), F32), jnp.zeros((8, lanes), F32)]
    for k, hit in enumerate(hits):
        rank = jnp.sum(jnp.where(hit, before, 0.0), axis=0, keepdims=True)
        to = routes[k:k + 1].astype(jnp.int32)
        ec, ez, ey = lax.rem(to, 2), lax.rem(to // 2, n), to // (2 * n)
        by_y = (ey * (2 * n) + ez * 2 + ec) * ch + (y * 2 + c + 1)
        by_z = (ez * (2 * n) + ey * 2 + ec) * ch + (z * 2 + c + 1)
        for mode, place in enumerate((by_y, by_z)):
            code = jnp.where(held, place.astype(F32) + rank * (2.0 * n), 0.0)
            picks[mode] = jnp.where(level == k, code, picks[mode])
            picks[mode] = jnp.where(level == 4 + k, gates[k:k + 1], picks[mode])
    info[0] = picks[0]
    info[1] = picks[1]
    pl.semaphore_wait(barrier, 4 * n - 3 + 2)

    pending = []

    def go(copy):
        copy.start()
        pending.append(copy)
        return copy

    psib = jnp.where(first, z, y)
    mine = pl.ds(pl.multiple_of(c * tok, tok), tok)
    mycol = pl.ds(pl.multiple_of(c * wh, wh), wh)
    hiscol = pl.ds(pl.multiple_of((1 - c) * wh, wh), wh)
    swap = [
        go(remote(info.at[1 - c], infor, p0_s.at[2], p0_r.at[2], sib)),
        go(remote(x_ref.at[:, hiscol], buf.at[0, psib, mine], p0_s.at[0], p0_r.at[0], sib)),
        go(remote(dy_ref.at[:, hiscol], buf.at[1, psib, mine], p0_s.at[1], p0_r.at[1], sib)),
    ]

    wcopies = []
    for k, (src, dst) in enumerate(((wgu_ref, wgu), (wdn_ref, wdn))):
        wcopies.append(go(remote(src, dst.at[d], w_s.at[0, 0, k], w_r.at[0, 0, k], {"dp": right})))
        wcopies.append(go(remote(src, dst.at[d], w_s.at[0, 1, k], w_r.at[0, 1, k], {"dp": left})))
    buf[0, p, mine] = x_ref[:, mycol]
    buf[1, p, mine] = dy_ref[:, mycol]
    wgu[d] = wgu_ref[...]
    wdn[d] = wdn_ref[...]

    def ag(s, way, a):
        at = lax.rem(p - s + n, n) if way == 0 else lax.rem(p + s, n)
        ref = buf.at[a, at, pl.ds(way * tok, tok)] if s == half_n - 1 else buf.at[a, at]
        return remote(ref, ref, ag_s.at[way, s, a], ag_r.at[way, s, a], ring(1 if way == 0 else -1))

    copies = {}

    def gather(s):
        for a in range(2):
            if s == 0:
                swap[1 + a].wait_recv()
            for way in range(2):
                if s > 0:
                    copies[s - 1, way, a].wait_recv()
            for way in range(2):
                copies[s, way, a] = go(ag(s, way, a))

    swap[0].wait_recv()
    infob[p] = info[c] + infor[...]

    @pl.loop(1, n)
    def _(k):
        remote(infob.at[p], infob.at[p], in_s.at[k], in_r.at[p], ring(k)).start()

    gather(0)

    @pl.loop(1, n)
    def _(k):
        at = lax.rem(p + k, n)
        pltpu.make_async_copy(infob.at[at], infob.at[at], in_r.at[at]).wait()

    if half_n > 1:
        gather(1)

    @pl.loop(0, n)
    def _(at):
        block = infob[at]
        rows = lax.broadcasted_iota(jnp.int32, (2 * n * ch, lanes), 0).astype(F32)
        picked = jnp.zeros((2 * n * ch, lanes), F32)
        scaled = jnp.zeros((2 * n * ch, lanes), F32)
        for k in range(4):
            hit = rows == (block[k:k + 1, :] - base)
            picked = jnp.where(hit, 1.0, picked)
            scaled = jnp.where(hit, block[4 + k:5 + k, :], scaled)
        cols = pl.ds(pl.multiple_of(at * lanes, lanes), lanes)
        sel[0, :, cols] = picked.astype(BF)
        sel[1, :, cols] = scaled.astype(BF)

    for s in range(2, half_n):
        gather(s)

    def dispatch(a):
        for way in range(2):
            copies[half_n - 1, way, a].wait_recv()

        @pl.loop(0, half_n)
        def _(g):
            places = (lax.rem(bm + g, n), lax.rem(bm + g + half_n, n))
            spans = [pl.ds(pl.multiple_of(b * (2 * ch), 2 * ch), 2 * ch) for b in places]
            lhs = jnp.concatenate([sel[a, span, :] for span in spans], axis=0)
            rows = dot(lhs, buf[a].reshape(n * lanes, wh)).astype(BF)
            for i, (b, span) in enumerate(zip(places, spans)):
                sb[a, span, :] = rows[i * 2 * ch:(i + 1) * 2 * ch]
                for cc in range(2):
                    src = sb.at[a, pl.ds(pl.multiple_of((b * 2 + cc) * ch, ch), ch)]
                    dst = xs.at[a, c, pl.ds(pl.multiple_of(bm * ch, ch), ch)]
                    own = jnp.logical_and(b == bm, c == cc)

                    @pl.when(own)
                    def _():
                        pltpu.make_async_copy(src, dst, a2_r.at[a, c, bm]).start()

                    @pl.when(jnp.logical_not(own))
                    def _():
                        remote(src, dst, a2_s.at[a, b * 2 + cc], a2_r.at[a, c, bm], other(b, cc)).start()

    def arrived(a):
        @pl.loop(0, n)
        def _(b):
            for h in range(2):
                ref = xs.at[a, h, pl.ds(pl.multiple_of(b * ch, ch), ch)]
                pltpu.make_async_copy(ref, ref, a2_r.at[a, h, b]).wait()

        xs[a, 1] = dot(perm_ref[...], xs[a, 1]).astype(BF)

    dispatch(0)
    dispatch(1)
    halfb = blk // 2
    for copy in wcopies:
        copy.wait_recv()
    wc2 = []
    for k, dst in enumerate((wgu, wdn)):
        top, low = dst.at[left, pl.ds(0, halfb)], dst.at[right, pl.ds(halfb, halfb)]
        wc2.append(go(remote(top, top, w_s.at[1, 0, k], w_r.at[1, 0, k], {"dp": right})))
        wc2.append(go(remote(low, low, w_s.at[1, 1, k], w_r.at[1, 1, k], {"dp": left})))

    def part(t):
        per = wh // blk
        return t // per, pl.ds(pl.multiple_of(lax.rem(t, per) * blk, blk), blk)

    arrived(0)
    blocks = []
    for k in range(3):
        to = lax.rem(d + k + 1, dpn)
        h, cols = part(to)
        blocks.append(go(remote(xs.at[0, h, :, cols], xa.at[d], xb_s.at[k], xb_r.at[k], {"dp": to})))
    for copy in wc2:
        copy.wait_recv()
    wgu_h = [wgu[h * dpn // 2:(h + 1) * dpn // 2].reshape(wh, 2 * hid) for h in range(2)]
    wdn_h = [wdn[h * dpn // 2:(h + 1) * dpn // 2].reshape(wh, hid) for h in range(2)]
    pre_s[...] = dot(xs[0, 0], wgu_h[0]) + dot(xs[0, 1], wgu_h[1])
    arrived(1)
    gh = dot(xs[1, 0], wdn_h[0]) + dot(xs[1, 1], wdn_h[1])
    gate, up = pre_s[:, :hid], pre_s[:, hid:]
    sig = jax.nn.sigmoid(gate)
    act = gate * sig
    hidden = (act * up).astype(BF)
    hid_s[...] = hidden
    gp_s[:, :hid] = (gh * up * sig * (1.0 + gate * (1.0 - sig))).astype(BF)
    gp_s[:, hid:] = (gh * act).astype(BF)
    bulk = [go(remote(gp_s, gpa.at[d], gp_sem_s.at[0, way], gp_sem_r.at[0, way], {"dp": to}))
            for way, to in ((0, right), (1, left))]
    weight_grad = jnp.sum(hidden.astype(F32) * gh, axis=1, keepdims=True)
    ranks = weight_grad.reshape(n, cap, 2 * n, 1)
    lane = lax.broadcasted_iota(jnp.int32, (n, 2 * n, LANES), 2)
    packed = jnp.zeros((n, 2 * n, LANES), F32)
    for r in range(cap):
        packed = jnp.where(lane == r, ranks[:, r], packed)
    g_out[...] = packed.astype(BF)

    def down_part(t):
        h, cols = part(t)
        return dot(xs[1, h, :, cols], hid_s[...], ((0,), (0,)))

    both = ((0, {"dp": right}, 0), (1, {"dp": left}, halfb))
    d0[...] = down_part(lax.rem(d + 2, dpn)).astype(BF)
    far_copies = [go(remote(d0.at[pl.ds(off, halfb)], r0.at[way], dp_s.at[0, way], dp_r.at[0, way], to))
                  for way, to, off in both]

    for h in range(2):
        rows = dot(gp_s[...], wgu_h[h], ((1,), (1,))).astype(BF)
        if h == 1:
            rows = dot(perm_ref[...], rows).astype(BF)
        ret[h] = rows

        @pl.loop(0, n)
        def _(i):
            b = lax.rem(bm + i, n)
            src = ret.at[h, pl.ds(pl.multiple_of(b * ch, ch), ch)]
            q = (z if h == 0 else y) * 2 + c
            dst = back.at[pl.ds(pl.multiple_of(q * ch, ch), ch)]
            own = jnp.logical_and(c == h, b == bm)

            @pl.when(own)
            def _():
                pltpu.make_async_copy(src, dst, bk_r.at[q]).start()

            @pl.when(jnp.logical_not(own))
            def _():
                to = dev(y, b, 0) if h == 0 else dev(b, z, 1)
                remote(src, dst, bk_s.at[h, b], bk_r.at[q], to).start()

    @pl.loop(0, n)
    def _(b):
        own = jnp.logical_and(first, b == bm)

        @pl.when(own)
        def _():
            pltpu.make_async_copy(g_out.at[b], g_in.at[z * 2 + c], gb_r.at[z * 2 + c]).start()

        @pl.when(jnp.logical_not(own))
        def _():
            remote(g_out.at[b], g_in.at[z * 2 + c], gb_s.at[b], gb_r.at[z * 2 + c], dev(y, b, 0)).start()

    here_h, here_cols = part(d)
    ddn_ref[...] = down_part(d)
    dgu_ref[...] = dot(xs[0, here_h, :, here_cols], gp_s[...], ((0,), (0,)))
    near = []
    for way, to, off in both:
        dn = down_part(right if way == 0 else left)
        far_copies[way].wait_recv()
        d1[way] = dn.astype(BF)
        here = slice(off, off + halfb)
        d1[way, here] = (dn[here] + r0[way].astype(F32)).astype(BF)
        near.append(go(remote(d1.at[way], r1.at[way], dp_s.at[1, way], dp_r.at[1, way], to)))
    half_rows = n * ch // 2
    for copy in bulk:
        copy.wait_recv()
    top, low = gpa.at[left, pl.ds(0, half_rows)], gpa.at[right, pl.ds(half_rows, half_rows)]
    rest = [go(remote(top, top, gp_sem_s.at[1, 0], gp_sem_r.at[1, 0], {"dp": right})),
            go(remote(low, low, gp_sem_s.at[1, 1], gp_sem_r.at[1, 1], {"dp": left}))]

    def add_block(t):
        dgu_ref[...] += dot(xa[t], gpa[t], ((0,), (0,)))

    @pl.loop(0, 2 * n)
    def _(q):
        ref = back.at[pl.ds(pl.multiple_of(q * ch, ch), ch)]
        pltpu.make_async_copy(ref, ref, bk_r.at[q]).wait()

    def share(t):
        cols = pl.ds(pl.multiple_of(t * lanes, lanes), lanes)
        return dot(sel[0, :, cols], back[...], ((0,), (0,)))

    pieces = 4
    piece = lanes // pieces

    def rows_of(m):
        return slice(m * piece, (m + 1) * piece)

    def rs(s, way, m):
        rows = pl.ds(m * piece, piece)
        return remote(rs_out.at[way, s, rows], rs_in.at[way, s, rows],
                      rs_s.at[way, s, m], rs_r.at[way, s, m], ring(1 if way == 0 else -1))

    def rs_runs(s, way, m):
        return s > 0 or m // (pieces // 2) == way

    whole = share(lax.rem(p + half_n, n)).astype(BF)
    rcopies = {}
    for m in range(pieces):
        for way in range(2):
            if rs_runs(0, way, m):
                rs_out[way, 0, rows_of(m)] = whole[rows_of(m)]
                rcopies[0, way, m] = go(rs(0, way, m))

    @pl.when(first)
    def _():
        @pl.loop(0, 2 * n)
        def _(q):
            pltpu.make_async_copy(g_in.at[q], g_in.at[q], gb_r.at[q]).wait()

        lane3 = lax.broadcasted_iota(jnp.int32, (2 * n, 2 * n, LANES), 2)
        packed_in = g_in[...].astype(F32)
        for r in range(cap):
            value = jnp.sum(jnp.where(lane3 == r, packed_in, 0.0), axis=2, keepdims=True)
            g_col[:, r] = jnp.broadcast_to(value, (2 * n, 2 * n, lanes))

        @pl.loop(0, n)
        def _(i):
            at = lax.rem(p + i, n)
            block = infob[at]
            rows = lax.broadcasted_iota(jnp.int32, (2 * n * ch, lanes), 0).astype(F32)
            column = g_col[...].reshape(2 * n * ch, lanes)
            tile = jnp.zeros((8, lanes), F32)
            for k in range(4):
                hit = rows == (block[k:k + 1, :] - base)
                found = jnp.sum(jnp.where(hit, column, 0.0), axis=0, keepdims=True)
                tile = jnp.where(level == k, found, tile)
            g_part[at] = tile

            @pl.when(i == 0)
            def _():
                pltpu.make_async_copy(g_part.at[at], g_all.at[p], gs_r.at[p]).start()

            @pl.when(i != 0)
            def _():
                remote(g_part.at[at], g_all.at[p], gs_s.at[at], gs_r.at[p], dev(at, z, 0)).start()

    def taken(s, way, m, held_part):
        if not rs_runs(s, way, m):
            return held_part
        rcopies[s, way, m].wait_recv()
        return held_part + rs_in[way, s, rows_of(m)].astype(F32)

    for s in range(1, half_n):
        shares = [share(lax.rem(p + half_n - s if way == 0 else p + half_n + s, n)) for way in range(2)]
        for m in range(pieces):
            for way in range(2):
                rs_out[way, s, rows_of(m)] = taken(s - 1, way, m, shares[way][rows_of(m)]).astype(BF)
                rcopies[s, way, m] = go(rs(s, way, m))
        if s == 1:
            for copy in blocks:
                copy.wait_recv()
            add_block(left)
        if s == 2:
            add_block(right)
    total = share(p)
    for m in range(pieces):
        value = taken(half_n - 1, 0, m, total[rows_of(m)])
        fin[rows_of(m)] = taken(half_n - 1, 1, m, value).astype(BF)
    his = pl.ds(pl.multiple_of((1 - c) * tok, tok), tok)
    swapped = go(remote(fin.at[his], finr, f_s, f_r, sib))
    gt_ref[:, mycol] = fin[mine, :]

    @pl.when(first)
    def _():
        g_sum = jnp.zeros((8, lanes), F32)
        for src in range(n):
            pltpu.make_async_copy(g_all.at[src], g_all.at[src], gs_r.at[src]).wait()
            g_sum = g_sum + g_all[src]
        g_fin[...] = g_sum
        remote(g_fin, g_part.at[0], gf_s, gf_r, sib).start()

    swapped.wait_recv()
    gt_ref[:, hiscol] = finr[...]

    for copy in near:
        copy.wait_recv()
    ddn_ref[...] += r1[0].astype(F32) + r1[1].astype(F32)
    for copy in rest:
        copy.wait_recv()
    if half_n < 3:
        for copy in blocks[:3 if half_n < 2 else 0]:
            copy.wait_recv()
        for t in (left, right)[half_n - 1:]:
            add_block(t)
    add_block(lax.rem(d + 2, dpn))

    @pl.when(first)
    def _():
        pltpu.make_async_copy(g_fin, g_fin, gf_s).wait()

        @pl.loop(1, n)
        def _(i):
            at = lax.rem(p + i, n)
            pltpu.make_async_copy(g_part.at[at], g_part.at[at], gs_s.at[at]).wait()

    @pl.when(c == 1)
    def _():
        pltpu.make_async_copy(g_fin, g_fin, gf_r).wait()
        g_fin[...] = g_part[0]

    quotient = jnp.where(held, g_fin[0:4], 0.0) / jnp.where(held, info[0, 4:8], 1.0)
    gr_ref[...] = dot(quotient.astype(BF), spread, ((1,), (1,))).astype(BF)

    for copy in pending:
        copy.wait_send()

    @pl.loop(1, n)
    def _(k):
        pltpu.make_async_copy(infob.at[p], infob.at[p], in_s.at[k]).wait()

    @pl.loop(0, n)
    def _(b):
        for a in range(2):
            for cc in range(2):
                @pl.when(jnp.logical_not(jnp.logical_and(b == bm, c == cc)))
                def _():
                    ref = sb.at[a, pl.ds(pl.multiple_of((b * 2 + cc) * ch, ch), ch)]
                    pltpu.make_async_copy(ref, ref, a2_s.at[a, b * 2 + cc]).wait()
        for h in range(2):
            @pl.when(jnp.logical_not(jnp.logical_and(c == h, b == bm)))
            def _():
                ref = ret.at[h, pl.ds(pl.multiple_of(b * ch, ch), ch)]
                pltpu.make_async_copy(ref, ref, bk_s.at[h, b]).wait()
                if h == 0:
                    pltpu.make_async_copy(g_out.at[b], g_out.at[b], gb_s.at[b]).wait()


def on_device(n, dpn, tokens, grad_out, route_expert, route_weight, gate_up_weight, down_weight):
    tok, width = tokens.shape
    top = route_expert.shape[1]
    wh = width // 2
    blk, hid = down_weight.shape[1:]
    experts = 2 * n * n
    cap = min(tok, (tok * top + experts - 1) // experts + 1)
    ch = 2 * n * cap
    lanes = 2 * tok
    at = np.arange(n * ch)
    hop = (at % (2 * n)) // 2 * ch + (at % ch) // (2 * n) * (2 * n) + at // ch * 2 + at % 2
    perm = np.zeros((n * ch, n * ch), np.float32)
    perm[at, hop] = 1.0
    perm = jnp.asarray(perm, BF)

    vm = pl.BlockSpec(memory_space=pltpu.VMEM)
    half_n = n // 2
    dma = pltpu.SemaphoreType.DMA
    all_rows = 2 * n * ch
    wx = wh
    scratch = [
        pltpu.VMEM((2, n, lanes, wh), BF),
        pltpu.VMEM((2, 8, lanes), F32),
        pltpu.VMEM((n, 8, lanes), F32),
        pltpu.VMEM((8, lanes), F32),
        pltpu.VMEM((2, all_rows, n * lanes), BF),
        pltpu.VMEM((2, all_rows, wh), BF),
        pltpu.VMEM((2, 2, n * ch, wh), BF),
        pltpu.VMEM((dpn, blk, 2 * hid), BF),
        pltpu.VMEM((dpn, blk, hid), BF),
        pltpu.VMEM((n * ch, 2 * hid), F32),
        pltpu.VMEM((n * ch, 2 * hid), BF),
        pltpu.VMEM((n * ch, hid), BF),
        pltpu.VMEM((2, n * ch, wx), BF),
        pltpu.VMEM((all_rows, wx), BF),
        pltpu.VMEM((2, half_n, lanes, wx), BF),
        pltpu.VMEM((2, half_n, lanes, wx), BF),
        pltpu.VMEM((lanes, wx), BF),
        pltpu.VMEM((tok, wx), BF),
        pltpu.VMEM((blk, hid), BF),
        pltpu.VMEM((2, blk, hid), BF),
        pltpu.VMEM((2, blk // 2, hid), BF),
        pltpu.VMEM((2, blk, hid), BF),
        pltpu.VMEM((dpn, n * ch, blk), BF),
        pltpu.VMEM((dpn, n * ch, 2 * hid), BF),
        pltpu.VMEM((n, 2 * n, LANES), BF),
        pltpu.VMEM((2 * n, 2 * n, LANES), BF),
        pltpu.VMEM((2 * n, cap, 2 * n, lanes), F32),
        pltpu.VMEM((n, 8, lanes), F32),
        pltpu.VMEM((n, 8, lanes), F32),
        pltpu.VMEM((8, lanes), F32),
        dma((3,)), dma((3,)),
        dma((2, half_n, 2)), dma((2, half_n, 2)),
        dma((n,)), dma((n,)),
        dma((2, 2 * n)), dma((2, 2, n)),
        dma((2, 2, 2)), dma((2, 2, 2)),
        dma((2, n)), dma((2 * n,)),
        dma((2, half_n, 4)), dma((2, half_n, 4)),
        dma, dma,
        dma((2, 2)), dma((2, 2)),
        dma((n,)), dma((2 * n,)),
        dma((n,)), dma((n,)),
        dma, dma,
        dma((3,)), dma((3,)),
        dma((2, 2)), dma((2, 2)),
    ]
    grad_tokens, grad_w, grad_gu, grad_dn = pl.pallas_call(
        functools.partial(kernel, n, cap, dpn),
        out_shape=(
            jax.ShapeDtypeStruct((tok, width), BF),
            jax.ShapeDtypeStruct((top, tok), BF),
            jax.ShapeDtypeStruct((blk, 2 * hid), F32),
            jax.ShapeDtypeStruct((blk, hid), F32),
        ),
        in_specs=[vm] * 7,
        out_specs=(vm, vm, vm, vm),
        scratch_shapes=scratch,
        compiler_params=pltpu.CompilerParams(
            collective_id=0, has_side_effects=True, vmem_limit_bytes=60 * 1024 * 1024),
    )(tokens, grad_out, route_expert.T, route_weight.T, perm, gate_up_weight[0], down_weight[0])
    grad_route = grad_w.T
    return grad_tokens, grad_route, grad_gu[None], grad_dn[None]


def solution(mesh):
    n = math.isqrt(mesh.shape["expert"] // 2)
    return jax.shard_map(
        functools.partial(on_device, n, mesh.shape["dp"]),
        mesh=mesh,
        in_specs=(
            P(("expert", "dp"), None),
            P(("expert", "dp"), None),
            P(("expert", "dp"), None),
            P(("expert", "dp"), None),
            P("expert", "dp", None),
            P("expert", "dp", None),
        ),
        out_specs=(
            P(("expert", "dp"), None),
            P(("expert", "dp"), None),
            P("expert", "dp", None),
            P("expert", "dp", None),
        ),
        check_vma=False,
    )
```

```python
import functools
import math

import jax
import jax.numpy as jnp
import numpy as np
from jax import lax
from jax.experimental import pallas as pl
from jax.experimental.pallas import tpu as pltpu
from jax.sharding import PartitionSpec as P

BF = jnp.bfloat16
F32 = jnp.float32
LANES = 128


def dot(a, b, dims=((1,), (0,))):
    return lax.dot_general(a, b, (dims, ((), ())), preferred_element_type=F32)


def kernel(n, cap, dpn, x_ref, dy_ref, route_ref, weight_ref, perm_ref, wgu_ref, wdn_ref,
           gt_ref, gr_ref, dgu_ref, ddn_ref,
           buf, info, infob, infor, sel, sb, xs, wgu, wdn, pre_s, gp_s, hid_s, ret, back,
           rs_out, rs_in, fin, finr, d0, d1, r0, r1, xa, gpa, g_out, g_in, g_col, g_part, g_all, g_fin,
           p0_s, p0_r, ag_s, ag_r, in_s, in_r, a2_s, a2_r, w_s, w_r, bk_s, bk_r, rs_s, rs_r,
           f_s, f_r, dp_s, dp_r, gb_s, gb_r, gs_s, gs_r, gf_s, gf_r, xb_s, xb_r, gp_sem_s, gp_sem_r, perm, ld, last_in, last_r, dgu_v, out_s, fs_s, fs_r):
    half_n = n // 2
    ch = 2 * n * cap
    tok, width = x_ref.shape
    wh = width // 2
    hid = wdn_ref.shape[1]
    blk = wgu_ref.shape[0]
    e = lax.axis_index("expert")
    d = lax.axis_index("dp")
    c = lax.rem(e, 2)
    z = lax.rem(e // 2, n)
    y = e // (2 * n)
    first = c == 0
    p = jnp.where(first, y, z)
    bm = jnp.where(first, z, y)

    def dev(yy, zz, cc):
        return {"expert": (yy * n + zz) * 2 + cc}

    def ring(k):
        at = lax.rem(p + k + n, n)
        return {"expert": jnp.where(first, (at * n + z) * 2, (y * n + at) * 2 + 1)}

    def other(b, cc):
        return {"expert": jnp.where(first, (y * n + b) * 2 + cc, (b * n + z) * 2 + cc)}

    sib = dev(y, z, 1 - c)
    right, left = lax.rem(d + 1, dpn), lax.rem(d + dpn - 1, dpn)

    def remote(src, dst, ss, rs, to):
        return pltpu.make_async_remote_copy(
            src_ref=src, dst_ref=dst, send_sem=ss, recv_sem=rs, device_id=to,
            device_id_type=pl.DeviceIdType.MESH)

    fetch = [pltpu.make_async_copy(src, dst, at_sem) for src, dst, at_sem in (
        (wgu_ref, wgu.at[d], ld.at[0]), (wdn_ref, wdn.at[d], ld.at[1]), (perm_ref, perm, ld.at[2]))]
    barrier = pltpu.get_barrier_semaphore()

    def greet(to):
        pl.semaphore_signal(barrier, inc=1, device_id=to, device_id_type=pl.DeviceIdType.MESH)

    @pl.loop(0, n)
    def _(b):
        for cc in range(2):
            @pl.when(jnp.logical_not(jnp.logical_and(b == z, c == cc)))
            def _():
                greet(dev(y, b, cc))

            @pl.when(b != y)
            def _():
                greet(dev(b, z, cc))

    greet({"dp": right})
    greet({"dp": left})
    for copy in fetch:
        copy.start()

    experts = 2 * n * n
    lanes = 2 * tok
    base = (p * (n * 2 * ch) + 1).astype(F32)
    spot = lax.broadcasted_iota(jnp.int32, (tok, lanes), 1) - lax.broadcasted_iota(jnp.int32, (tok, lanes), 0)
    spread = jnp.where(spot == c * tok, 1.0, 0.0).astype(BF)
    lane = lax.broadcasted_iota(jnp.int32, (1, lanes), 1)
    held = jnp.logical_and(lane >= c * tok, lane < c * tok + tok)
    routes = dot(route_ref[...].astype(F32).astype(BF), spread)
    gates = dot(weight_ref[...], spread)
    routes = jnp.where(held, routes, -1.0)
    expert_row = lax.broadcasted_iota(jnp.int32, (experts, lanes), 0).astype(F32)
    hits = [routes[k:k + 1] == expert_row for k in range(4)]
    named = jnp.zeros((experts, lanes), F32)
    for hit in hits:
        named = jnp.where(hit, 1.0, named)
    earlier = (lax.broadcasted_iota(jnp.int32, (lanes, lanes), 0)
               < lax.broadcasted_iota(jnp.int32, (lanes, lanes), 1))
    before = dot(named.astype(BF), jnp.where(earlier, 1.0, 0.0).astype(BF))
    level = lax.broadcasted_iota(jnp.int32, (8, lanes), 0)
    picks = [jnp.zeros((8, lanes), F32), jnp.zeros((8, lanes), F32)]
    for k, hit in enumerate(hits):
        rank = jnp.sum(jnp.where(hit, before, 0.0), axis=0, keepdims=True)
        to = routes[k:k + 1].astype(jnp.int32)
        ec, ez, ey = lax.rem(to, 2), lax.rem(to // 2, n), to // (2 * n)
        by_y = (ey * (2 * n) + ez * 2 + ec) * ch + (y * 2 + c + 1)
        by_z = (ez * (2 * n) + ey * 2 + ec) * ch + (z * 2 + c + 1)
        for mode, place in enumerate((by_y, by_z)):
            code = jnp.where(held, place.astype(F32) + rank * (2.0 * n), 0.0)
            picks[mode] = jnp.where(level == k, code, picks[mode])
            picks[mode] = jnp.where(level == 4 + k, gates[k:k + 1], picks[mode])
    info[0] = picks[0]
    info[1] = picks[1]
    pl.semaphore_wait(barrier, 4 * n - 3 + 2)

    pending = []

    def go(copy):
        copy.start()
        pending.append(copy)
        return copy

    psib = jnp.where(first, z, y)
    mine = pl.ds(pl.multiple_of(c * tok, tok), tok)
    mycol = pl.ds(pl.multiple_of(c * wh, wh), wh)
    hiscol = pl.ds(pl.multiple_of((1 - c) * wh, wh), wh)
    def first_step(a, way, h):
        k = 1 if way == 0 else -1
        if h == 0:
            to, at, cols = ring(k), p, mycol
        else:
            zz, yy = lax.rem(z + k + n, n), lax.rem(y + k + n, n)
            to = {"expert": jnp.where(first, (y * n + zz) * 2 + 1, (yy * n + z) * 2)}
            at, cols = psib, hiscol
        src = (x_ref, dy_ref)[a].at[:, cols]
        return remote(src, buf.at[a, at, mine], fs_s.at[way, a, h], fs_r.at[way, a, c], to)

    slots = go(remote(info.at[1 - c], infor, p0_s.at[2], p0_r.at[2], sib))
    for a in range(2):
        for way in range(2):
            for h in range(2):
                go(first_step(a, way, h))
    swap = [
        slots,
        go(remote(x_ref.at[:, hiscol], buf.at[0, psib, mine], p0_s.at[0], p0_r.at[0], sib)),
        go(remote(dy_ref.at[:, hiscol], buf.at[1, psib, mine], p0_s.at[1], p0_r.at[1], sib)),
    ]

    wcopies = []
    for k, dst in enumerate((wgu, wdn)):
        fetch[k].wait()
        src = dst.at[d]
        wcopies.append(go(remote(src, dst.at[d], w_s.at[0, 0, k], w_r.at[0, 0, k], {"dp": right})))
        wcopies.append(go(remote(src, dst.at[d], w_s.at[0, 1, k], w_r.at[0, 1, k], {"dp": left})))
    buf[0, p, mine] = x_ref[:, mycol]
    buf[1, p, mine] = dy_ref[:, mycol]
    fetch[2].wait()

    def ag(s, way, a):
        at = lax.rem(p - s + n, n) if way == 0 else lax.rem(p + s, n)
        ref = buf.at[a, at, pl.ds(way * tok, tok)] if s == half_n - 1 else buf.at[a, at]
        return remote(ref, ref, ag_s.at[way, s, a], ag_r.at[way, s, a], ring(1 if way == 0 else -1))

    copies = {}

    def gather(s):
        for a in range(2):
            for way in range(2):
                if s == 1:
                    at = lax.rem(p + n - 1 if way == 0 else p + 1, n)
                    for m in range(2):
                        ref = buf.at[a, at, pl.ds(m * tok, tok)]
                        pltpu.make_async_copy(ref, ref, fs_r.at[way, a, m]).wait()
                else:
                    copies[s - 1, way, a].wait_recv()
            for way in range(2):
                copies[s, way, a] = go(ag(s, way, a))

    swap[0].wait_recv()
    infob[p] = info[c] + infor[...]

    @pl.loop(1, n)
    def _(k):
        remote(infob.at[p], infob.at[p], in_s.at[k], in_r.at[p], ring(k)).start()

    gather(1)

    @pl.loop(1, n)
    def _(k):
        at = lax.rem(p + k, n)
        pltpu.make_async_copy(infob.at[at], infob.at[at], in_r.at[at]).wait()

    @pl.loop(0, n)
    def _(at):
        block = infob[at]
        rows = lax.broadcasted_iota(jnp.int32, (2 * n * ch, lanes), 0).astype(F32)
        picked = jnp.zeros((2 * n * ch, lanes), F32)
        scaled = jnp.zeros((2 * n * ch, lanes), F32)
        for k in range(4):
            hit = rows == (block[k:k + 1, :] - base)
            picked = jnp.where(hit, 1.0, picked)
            scaled = jnp.where(hit, block[4 + k:5 + k, :], scaled)
        cols = pl.ds(pl.multiple_of(at * lanes, lanes), lanes)
        sel[0, :, cols] = picked.astype(BF)
        sel[1, :, cols] = scaled.astype(BF)

    for s in range(2, half_n):
        gather(s)

    def dispatch(a):
        swap[1 + a].wait_recv()
        for way in range(2):
            copies[half_n - 1, way, a].wait_recv()

        @pl.loop(0, half_n)
        def _(g):
            places = (lax.rem(bm + g, n), lax.rem(bm + g + half_n, n))
            spans = [pl.ds(pl.multiple_of(b * (2 * ch), 2 * ch), 2 * ch) for b in places]
            lhs = jnp.concatenate([sel[a, span, :] for span in spans], axis=0)
            rows = dot(lhs, buf[a].reshape(n * lanes, wh)).astype(BF)
            for i, (b, span) in enumerate(zip(places, spans)):
                sb[a, span, :] = rows[i * 2 * ch:(i + 1) * 2 * ch]
                for cc in range(2):
                    src = sb.at[a, pl.ds(pl.multiple_of((b * 2 + cc) * ch, ch), ch)]
                    dst = xs.at[a, c, pl.ds(pl.multiple_of(bm * ch, ch), ch)]
                    own = jnp.logical_and(b == bm, c == cc)

                    @pl.when(own)
                    def _():
                        pltpu.make_async_copy(src, dst, a2_r.at[a, c, bm]).start()

                    @pl.when(jnp.logical_not(own))
                    def _():
                        remote(src, dst, a2_s.at[a, b * 2 + cc], a2_r.at[a, c, bm], other(b, cc)).start()

    def arrived(a):
        @pl.loop(0, n)
        def _(b):
            for h in range(2):
                ref = xs.at[a, h, pl.ds(pl.multiple_of(b * ch, ch), ch)]
                pltpu.make_async_copy(ref, ref, a2_r.at[a, h, b]).wait()

        xs[a, 1] = dot(perm[...], xs[a, 1]).astype(BF)

    dispatch(0)
    dispatch(1)
    halfb = blk // 2
    for copy in wcopies:
        copy.wait_recv()
    wc2 = []
    for k, dst in enumerate((wgu, wdn)):
        top, low = dst.at[left, pl.ds(0, halfb)], dst.at[right, pl.ds(halfb, halfb)]
        wc2.append(go(remote(top, top, w_s.at[1, 0, k], w_r.at[1, 0, k], {"dp": right})))
        wc2.append(go(remote(low, low, w_s.at[1, 1, k], w_r.at[1, 1, k], {"dp": left})))

    def part(t):
        per = wh // blk
        return t // per, pl.ds(pl.multiple_of(lax.rem(t, per) * blk, blk), blk)

    arrived(0)
    blocks = []
    for k in range(3):
        to = lax.rem(d + k + 1, dpn)
        h, cols = part(to)
        blocks.append(go(remote(xs.at[0, h, :, cols], xa.at[d], xb_s.at[k], xb_r.at[k], {"dp": to})))
    for copy in wc2:
        copy.wait_recv()
    wgu_h = [wgu[h * dpn // 2:(h + 1) * dpn // 2].reshape(wh, 2 * hid) for h in range(2)]
    wdn_h = [wdn[h * dpn // 2:(h + 1) * dpn // 2].reshape(wh, hid) for h in range(2)]
    pre_s[...] = dot(xs[0, 0], wgu_h[0]) + dot(xs[0, 1], wgu_h[1])
    arrived(1)
    gh = dot(xs[1, 0], wdn_h[0]) + dot(xs[1, 1], wdn_h[1])
    gate, up = pre_s[:, :hid], pre_s[:, hid:]
    sig = jax.nn.sigmoid(gate)
    act = gate * sig
    hidden = (act * up).astype(BF)
    hid_s[...] = hidden
    gp_s[:, :hid] = (gh * up * sig * (1.0 + gate * (1.0 - sig))).astype(BF)
    gp_s[:, hid:] = (gh * act).astype(BF)
    bulk = [go(remote(gp_s, gpa.at[d], gp_sem_s.at[0, way], gp_sem_r.at[0, way], {"dp": to}))
            for way, to in ((0, right), (1, left))]
    weight_grad = jnp.sum(hidden.astype(F32) * gh, axis=1, keepdims=True)
    ranks = weight_grad.reshape(n, cap, 2 * n, 1)
    lane = lax.broadcasted_iota(jnp.int32, (n, 2 * n, LANES), 2)
    packed = jnp.zeros((n, 2 * n, LANES), F32)
    for r in range(cap):
        packed = jnp.where(lane == r, ranks[:, r], packed)
    g_out[...] = packed.astype(BF)

    def down_part(t):
        h, cols = part(t)
        return dot(xs[1, h, :, cols], hid_s[...], ((0,), (0,)))

    both = ((0, {"dp": right}, 0), (1, {"dp": left}, halfb))
    d0[...] = down_part(lax.rem(d + 2, dpn)).astype(BF)
    far_copies = [go(remote(d0.at[pl.ds(off, halfb)], r0.at[way], dp_s.at[0, way], dp_r.at[0, way], to))
                  for way, to, off in both]

    for h in range(2):
        rows = dot(gp_s[...], wgu_h[h], ((1,), (1,))).astype(BF)
        if h == 1:
            rows = dot(perm[...], rows).astype(BF)
        ret[h] = rows

        @pl.loop(0, n)
        def _(i):
            b = lax.rem(bm + i, n)
            src = ret.at[h, pl.ds(pl.multiple_of(b * ch, ch), ch)]
            q = (z if h == 0 else y) * 2 + c
            dst = back.at[pl.ds(pl.multiple_of(q * ch, ch), ch)]
            own = jnp.logical_and(c == h, b == bm)

            @pl.when(own)
            def _():
                pltpu.make_async_copy(src, dst, bk_r.at[q]).start()

            @pl.when(jnp.logical_not(own))
            def _():
                to = dev(y, b, 0) if h == 0 else dev(b, z, 1)
                remote(src, dst, bk_s.at[h, b], bk_r.at[q], to).start()

    @pl.loop(0, n)
    def _(b):
        own = jnp.logical_and(first, b == bm)

        @pl.when(own)
        def _():
            pltpu.make_async_copy(g_out.at[b], g_in.at[z * 2 + c], gb_r.at[z * 2 + c]).start()

        @pl.when(jnp.logical_not(own))
        def _():
            remote(g_out.at[b], g_in.at[z * 2 + c], gb_s.at[b], gb_r.at[z * 2 + c], dev(y, b, 0)).start()

    here_h, here_cols = part(d)
    ddn_ref[...] = down_part(d)
    dgu_v[...] = dot(xs[0, here_h, :, here_cols], gp_s[...], ((0,), (0,)))
    half_rows = n * ch // 2
    for copy in bulk:
        copy.wait_recv()
    top, low = gpa.at[left, pl.ds(0, half_rows)], gpa.at[right, pl.ds(half_rows, half_rows)]
    rest = [go(remote(top, top, gp_sem_s.at[1, 0], gp_sem_r.at[1, 0], {"dp": right})),
            go(remote(low, low, gp_sem_s.at[1, 1], gp_sem_r.at[1, 1], {"dp": left}))]

    near = []
    for way, to, off in both:
        dn = down_part(right if way == 0 else left)
        far_copies[way].wait_recv()
        d1[way] = dn.astype(BF)
        here = slice(off, off + halfb)
        d1[way, here] = (dn[here] + r0[way].astype(F32)).astype(BF)
        near.append(go(remote(d1.at[way], r1.at[way], dp_s.at[1, way], dp_r.at[1, way], to)))
    def add_block(t):
        dgu_v[...] += dot(xa[t], gpa[t], ((0,), (0,)))

    @pl.loop(0, 2 * n)
    def _(q):
        ref = back.at[pl.ds(pl.multiple_of(q * ch, ch), ch)]
        pltpu.make_async_copy(ref, ref, bk_r.at[q]).wait()

    def share(t):
        cols = pl.ds(pl.multiple_of(t * lanes, lanes), lanes)
        return dot(sel[0, :, cols], back[...], ((0,), (0,)))

    pieces = 4
    piece = lanes // pieces

    def rows_of(m):
        return slice(m * piece, (m + 1) * piece)

    def rs(s, way, m):
        rows = pl.ds(m * piece, piece)
        k = 1 if way == 0 else -1
        if s < half_n - 1:
            return remote(rs_out.at[way, s, rows], rs_in.at[way, s, rows],
                          rs_s.at[way, s, m], rs_r.at[way, s, m], ring(k))
        at = lax.rem(p + k + n, n)
        owner = m * 2 // pieces
        to = {"expert": jnp.where(first, (at * n + z) * 2, (y * n + at) * 2) + owner}
        i = m % (pieces // 2)
        return remote(rs_out.at[way, s, rows], last_in.at[c, way, pl.ds(i * piece, piece)],
                      rs_s.at[way, s, m], last_r.at[c, way, i], to)

    def rs_runs(s, way, m):
        return s > 0 or m // (pieces // 2) == way

    whole = share(lax.rem(p + half_n, n)).astype(BF)
    rcopies = {}
    for m in range(pieces):
        for way in range(2):
            if rs_runs(0, way, m):
                rs_out[way, 0, rows_of(m)] = whole[rows_of(m)]
                rcopies[0, way, m] = go(rs(0, way, m))

    @pl.when(first)
    def _():
        @pl.loop(0, 2 * n)
        def _(q):
            pltpu.make_async_copy(g_in.at[q], g_in.at[q], gb_r.at[q]).wait()

        lane3 = lax.broadcasted_iota(jnp.int32, (2 * n, 2 * n, LANES), 2)
        packed_in = g_in[...].astype(F32)
        for r in range(cap):
            value = jnp.sum(jnp.where(lane3 == r, packed_in, 0.0), axis=2, keepdims=True)
            g_col[:, r] = jnp.broadcast_to(value, (2 * n, 2 * n, lanes))

        @pl.loop(0, n)
        def _(i):
            at = lax.rem(p + i, n)
            block = infob[at]
            rows = lax.broadcasted_iota(jnp.int32, (2 * n * ch, lanes), 0).astype(F32)
            column = g_col[...].reshape(2 * n * ch, lanes)
            tile = jnp.zeros((8, lanes), F32)
            for k in range(4):
                hit = rows == (block[k:k + 1, :] - base)
                found = jnp.sum(jnp.where(hit, column, 0.0), axis=0, keepdims=True)
                tile = jnp.where(level == k, found, tile)
            g_part[at] = tile

            @pl.when(i == 0)
            def _():
                pltpu.make_async_copy(g_part.at[at], g_all.at[p], gs_r.at[p]).start()

            @pl.when(i != 0)
            def _():
                remote(g_part.at[at], g_all.at[p], gs_s.at[at], gs_r.at[p], dev(at, z, 0)).start()

    def taken(s, way, m, held_part):
        if not rs_runs(s, way, m):
            return held_part
        rcopies[s, way, m].wait_recv()
        return held_part + rs_in[way, s, rows_of(m)].astype(F32)

    for s in range(1, half_n):
        shares = [share(lax.rem(p + half_n - s if way == 0 else p + half_n + s, n)) for way in range(2)]
        for m in range(pieces):
            for way in range(2):
                rs_out[way, s, rows_of(m)] = taken(s - 1, way, m, shares[way][rows_of(m)]).astype(BF)
                rcopies[s, way, m] = go(rs(s, way, m))
        if s == 1:
            for copy in blocks:
                copy.wait_recv()
            add_block(left)
        if s == 2:
            add_block(right)
    fin[...] = share(p).astype(BF)
    his = pl.ds(pl.multiple_of((1 - c) * tok, tok), tok)
    swapped = go(remote(fin.at[his], finr, f_s, f_r, sib))
    swapped.wait_recv()

    def finish(h, way, i):
        there = last_in.at[h, way, pl.ds(i * piece, piece)]
        pltpu.make_async_copy(there, there, last_r.at[h, way, i]).wait()
        return last_in[h, way, i * piece:(i + 1) * piece].astype(F32)

    for i in range(pieces // 2):
        span = slice(i * piece, (i + 1) * piece)
        for h, cols, begun in ((c, mycol, fin[pl.ds(pl.multiple_of(c * tok + i * piece, piece), piece), :]),
                               (1 - c, hiscol, finr[span])):
            value = begun.astype(F32)
            for way in range(2):
                value = value + finish(h, way, i)
            gt_ref[span, cols] = value.astype(BF)

    @pl.when(first)
    def _():
        g_sum = jnp.zeros((8, lanes), F32)
        for src in range(n):
            pltpu.make_async_copy(g_all.at[src], g_all.at[src], gs_r.at[src]).wait()
            g_sum = g_sum + g_all[src]
        g_fin[...] = g_sum
        remote(g_fin, g_part.at[0], gf_s, gf_r, sib).start()

    for copy in rest:
        copy.wait_recv()
    if half_n < 3:
        add_block(right)
    add_block(lax.rem(d + 2, dpn))
    leaving = pltpu.make_async_copy(dgu_v, dgu_ref, out_s)
    leaving.start()
    for copy in near:
        copy.wait_recv()
    ddn_ref[...] += r1[0].astype(F32) + r1[1].astype(F32)

    @pl.when(first)
    def _():
        pltpu.make_async_copy(g_fin, g_fin, gf_s).wait()

        @pl.loop(1, n)
        def _(i):
            at = lax.rem(p + i, n)
            pltpu.make_async_copy(g_part.at[at], g_part.at[at], gs_s.at[at]).wait()

    @pl.when(c == 1)
    def _():
        pltpu.make_async_copy(g_fin, g_fin, gf_r).wait()
        g_fin[...] = g_part[0]

    quotient = jnp.where(held, g_fin[0:4], 0.0) / jnp.where(held, info[0, 4:8], 1.0)
    gr_ref[...] = dot(quotient.astype(BF), spread, ((1,), (1,))).astype(BF)

    leaving.wait()
    for copy in pending:
        copy.wait_send()

    @pl.loop(1, n)
    def _(k):
        pltpu.make_async_copy(infob.at[p], infob.at[p], in_s.at[k]).wait()

    @pl.loop(0, n)
    def _(b):
        for a in range(2):
            for cc in range(2):
                @pl.when(jnp.logical_not(jnp.logical_and(b == bm, c == cc)))
                def _():
                    ref = sb.at[a, pl.ds(pl.multiple_of((b * 2 + cc) * ch, ch), ch)]
                    pltpu.make_async_copy(ref, ref, a2_s.at[a, b * 2 + cc]).wait()
        for h in range(2):
            @pl.when(jnp.logical_not(jnp.logical_and(c == h, b == bm)))
            def _():
                ref = ret.at[h, pl.ds(pl.multiple_of(b * ch, ch), ch)]
                pltpu.make_async_copy(ref, ref, bk_s.at[h, b]).wait()
                if h == 0:
                    pltpu.make_async_copy(g_out.at[b], g_out.at[b], gb_s.at[b]).wait()


def hand_over(*refs):
    count = len(refs) // 4
    ins, outs, rooms = refs[:count], refs[count:2 * count], refs[2 * count:3 * count]
    sems = refs[3 * count:]
    moves = []
    for src, dst, room, (come, leave) in zip(ins, outs, rooms, [(s.at[0], s.at[1]) for s in sems]):
        rows = src.shape[0]
        step = rows // 4 if rows >= 64 else rows
        for i in range(0, rows, step):
            part = pl.ds(i, step)
            moves.append((pltpu.make_async_copy(src.at[part], room.at[part], come.at[i // step]),
                          pltpu.make_async_copy(room.at[part], dst.at[part], leave.at[i // step])))
    for come, _ in moves:
        come.start()
    for come, leave in moves:
        come.wait()
        leave.start()
    for _, leave in moves:
        leave.wait()


def on_device(n, dpn, tokens, grad_out, route_expert, route_weight, gate_up_weight, down_weight):
    tok, width = tokens.shape
    top = route_expert.shape[1]
    wh = width // 2
    blk, hid = down_weight.shape[1:]
    experts = 2 * n * n
    cap = min(tok, (tok * top + experts - 1) // experts + 1)
    ch = 2 * n * cap
    lanes = 2 * tok
    at = np.arange(n * ch)
    hop = (at % (2 * n)) // 2 * ch + (at % ch) // (2 * n) * (2 * n) + at // ch * 2 + at % 2
    perm = np.zeros((n * ch, n * ch), np.float32)
    perm[at, hop] = 1.0
    perm = jnp.asarray(perm, BF)

    vm = pl.BlockSpec(memory_space=pltpu.VMEM)
    half_n = n // 2
    dma = pltpu.SemaphoreType.DMA
    all_rows = 2 * n * ch
    wx = wh
    scratch = [
        pltpu.VMEM((2, n, lanes, wh), BF),
        pltpu.VMEM((2, 8, lanes), F32),
        pltpu.VMEM((n, 8, lanes), F32),
        pltpu.VMEM((8, lanes), F32),
        pltpu.VMEM((2, all_rows, n * lanes), BF),
        pltpu.VMEM((2, all_rows, wh), BF),
        pltpu.VMEM((2, 2, n * ch, wh), BF),
        pltpu.VMEM((dpn, blk, 2 * hid), BF),
        pltpu.VMEM((dpn, blk, hid), BF),
        pltpu.VMEM((n * ch, 2 * hid), F32),
        pltpu.VMEM((n * ch, 2 * hid), BF),
        pltpu.VMEM((n * ch, hid), BF),
        pltpu.VMEM((2, n * ch, wx), BF),
        pltpu.VMEM((all_rows, wx), BF),
        pltpu.VMEM((2, half_n, lanes, wx), BF),
        pltpu.VMEM((2, half_n, lanes, wx), BF),
        pltpu.VMEM((lanes, wx), BF),
        pltpu.VMEM((tok, wx), BF),
        pltpu.VMEM((blk, hid), BF),
        pltpu.VMEM((2, blk, hid), BF),
        pltpu.VMEM((2, blk // 2, hid), BF),
        pltpu.VMEM((2, blk, hid), BF),
        pltpu.VMEM((dpn, n * ch, blk), BF),
        pltpu.VMEM((dpn, n * ch, 2 * hid), BF),
        pltpu.VMEM((n, 2 * n, LANES), BF),
        pltpu.VMEM((2 * n, 2 * n, LANES), BF),
        pltpu.VMEM((2 * n, cap, 2 * n, lanes), F32),
        pltpu.VMEM((n, 8, lanes), F32),
        pltpu.VMEM((n, 8, lanes), F32),
        pltpu.VMEM((8, lanes), F32),
        dma((3,)), dma((3,)),
        dma((2, half_n, 2)), dma((2, half_n, 2)),
        dma((n,)), dma((n,)),
        dma((2, 2 * n)), dma((2, 2, n)),
        dma((2, 2, 2)), dma((2, 2, 2)),
        dma((2, n)), dma((2 * n,)),
        dma((2, half_n, 4)), dma((2, half_n, 4)),
        dma, dma,
        dma((2, 2)), dma((2, 2)),
        dma((n,)), dma((2 * n,)),
        dma((n,)), dma((n,)),
        dma, dma,
        dma((3,)), dma((3,)),
        dma((2, 2)), dma((2, 2)),
        pltpu.VMEM((n * ch, n * ch), BF),
        dma((3,)),
        pltpu.VMEM((2, 2, tok, wx), BF),
        dma((2, 2, 2)),
        pltpu.VMEM((blk, 2 * hid), F32),
        dma,
        dma((2, 2, 2)), dma((2, 2, 2)),
    ]
    grad_tokens, grad_w, grad_gu, grad_dn = pl.pallas_call(
        functools.partial(kernel, n, cap, dpn),
        out_shape=(
            jax.ShapeDtypeStruct((tok, width), BF),
            jax.ShapeDtypeStruct((top, tok), BF),
            jax.ShapeDtypeStruct((blk, 2 * hid), F32),
            jax.ShapeDtypeStruct((blk, hid), F32),
        ),
        in_specs=[vm] * 4 + [pl.BlockSpec(memory_space=pl.ANY)] * 3,
        out_specs=(vm, vm, pl.BlockSpec(memory_space=pl.ANY), vm),
        scratch_shapes=scratch,
        compiler_params=pltpu.CompilerParams(
            collective_id=0, has_side_effects=True, vmem_limit_bytes=60 * 1024 * 1024),
    )(tokens, grad_out, route_expert.T, route_weight.T, perm, gate_up_weight[0], down_weight[0])
    grad_route = grad_w.T
    results = (grad_tokens, grad_gu, grad_dn)
    hbm = pl.BlockSpec(memory_space=pl.ANY)
    grad_tokens, grad_gu, grad_dn = pl.pallas_call(
        hand_over,
        out_shape=tuple(jax.ShapeDtypeStruct(r.shape, r.dtype) for r in results),
        in_specs=[hbm] * 3,
        out_specs=(hbm,) * 3,
        scratch_shapes=[pltpu.VMEM(r.shape, r.dtype) for r in results] + [dma((2, 4))] * 3,
        compiler_params=pltpu.CompilerParams(vmem_limit_bytes=60 * 1024 * 1024),
    )(*results)
    return grad_tokens, grad_route, grad_gu[None], grad_dn[None]


def solution(mesh):
    n = math.isqrt(mesh.shape["expert"] // 2)
    return jax.shard_map(
        functools.partial(on_device, n, mesh.shape["dp"]),
        mesh=mesh,
        in_specs=(
            P(("expert", "dp"), None),
            P(("expert", "dp"), None),
            P(("expert", "dp"), None),
            P(("expert", "dp"), None),
            P("expert", "dp", None),
            P("expert", "dp", None),
        ),
        out_specs=(
            P(("expert", "dp"), None),
            P(("expert", "dp"), None),
            P("expert", "dp", None),
            P("expert", "dp", None),
        ),
        check_vma=False,
    )
```

```python
import functools
import math

import jax
import jax.numpy as jnp
import numpy as np
from jax import lax
from jax.experimental import pallas as pl
from jax.experimental.pallas import tpu as pltpu
from jax.sharding import PartitionSpec as P

BF = jnp.bfloat16
F32 = jnp.float32
LANES = 128


def dot(a, b, dims=((1,), (0,))):
    return lax.dot_general(a, b, (dims, ((), ())), preferred_element_type=F32)


def kernel(n, cap, dpn, x_ref, dy_ref, route_ref, weight_ref, perm_ref, wgu_ref, wdn_ref,
           gt_ref, gr_ref, dgu_ref, ddn_ref,
           buf, info, infob, infor, sel, sb, xs, wgu, wdn, pre_s, gp_s, hid_s, ret, back,
           rs_out, rs_in, fin, finr, d0, d1, r0, r1, xa, gpa, g_out, g_in, g_col, g_part, g_all, g_fin,
           p0_s, p0_r, ag_s, ag_r, in_s, in_r, a2_s, a2_r, w_s, w_r, bk_s, bk_r, rs_s, rs_r,
           f_s, f_r, dp_s, dp_r, gb_s, gb_r, gs_s, gs_r, gf_s, gf_r, xb_s, xb_r, gp_sem_s, gp_sem_r, perm, ld, last_in, last_r, dgu_v, out_s, fs_s, fs_r):
    half_n = n // 2
    ch = 2 * n * cap
    tok, width = x_ref.shape
    wh = width // 2
    hid = wdn_ref.shape[1]
    blk = wgu_ref.shape[0]
    e = lax.axis_index("expert")
    d = lax.axis_index("dp")
    c = lax.rem(e, 2)
    z = lax.rem(e // 2, n)
    y = e // (2 * n)
    first = c == 0
    p = jnp.where(first, y, z)
    bm = jnp.where(first, z, y)

    def dev(yy, zz, cc):
        return {"expert": (yy * n + zz) * 2 + cc}

    def ring(k):
        at = lax.rem(p + k + n, n)
        return {"expert": jnp.where(first, (at * n + z) * 2, (y * n + at) * 2 + 1)}

    def other(b, cc):
        return {"expert": jnp.where(first, (y * n + b) * 2 + cc, (b * n + z) * 2 + cc)}

    sib = dev(y, z, 1 - c)
    right, left = lax.rem(d + 1, dpn), lax.rem(d + dpn - 1, dpn)

    def remote(src, dst, ss, rs, to):
        return pltpu.make_async_remote_copy(
            src_ref=src, dst_ref=dst, send_sem=ss, recv_sem=rs, device_id=to,
            device_id_type=pl.DeviceIdType.MESH)

    fetch = [pltpu.make_async_copy(src, dst, at_sem) for src, dst, at_sem in (
        (wgu_ref, wgu.at[d], ld.at[0]), (wdn_ref, wdn.at[d], ld.at[1]), (perm_ref, perm, ld.at[2]))]
    barrier = pltpu.get_barrier_semaphore()

    def greet(to):
        pl.semaphore_signal(barrier, inc=1, device_id=to, device_id_type=pl.DeviceIdType.MESH)

    @pl.loop(0, n)
    def _(b):
        for cc in range(2):
            @pl.when(jnp.logical_not(jnp.logical_and(b == z, c == cc)))
            def _():
                greet(dev(y, b, cc))

            @pl.when(b != y)
            def _():
                greet(dev(b, z, cc))

    greet({"dp": right})
    greet({"dp": left})
    for copy in fetch:
        copy.start()

    experts = 2 * n * n
    lanes = 2 * tok
    base = (p * (n * 2 * ch) + 1).astype(F32)
    spot = lax.broadcasted_iota(jnp.int32, (tok, lanes), 1) - lax.broadcasted_iota(jnp.int32, (tok, lanes), 0)
    spread = jnp.where(spot == c * tok, 1.0, 0.0).astype(BF)
    lane = lax.broadcasted_iota(jnp.int32, (1, lanes), 1)
    held = jnp.logical_and(lane >= c * tok, lane < c * tok + tok)
    routes = dot(route_ref[...].astype(F32).astype(BF), spread)
    gates = dot(weight_ref[...], spread)
    routes = jnp.where(held, routes, -1.0)
    expert_row = lax.broadcasted_iota(jnp.int32, (experts, lanes), 0).astype(F32)
    hits = [routes[k:k + 1] == expert_row for k in range(4)]
    named = jnp.zeros((experts, lanes), F32)
    for hit in hits:
        named = jnp.where(hit, 1.0, named)
    earlier = (lax.broadcasted_iota(jnp.int32, (lanes, lanes), 0)
               < lax.broadcasted_iota(jnp.int32, (lanes, lanes), 1))
    before = dot(named.astype(BF), jnp.where(earlier, 1.0, 0.0).astype(BF))
    level = lax.broadcasted_iota(jnp.int32, (8, lanes), 0)
    picks = [jnp.zeros((8, lanes), F32), jnp.zeros((8, lanes), F32)]
    for k, hit in enumerate(hits):
        rank = jnp.sum(jnp.where(hit, before, 0.0), axis=0, keepdims=True)
        to = routes[k:k + 1].astype(jnp.int32)
        ec, ez, ey = lax.rem(to, 2), lax.rem(to // 2, n), to // (2 * n)
        by_y = (ey * (2 * n) + ez * 2 + ec) * ch + (y * 2 + c + 1)
        by_z = (ez * (2 * n) + ey * 2 + ec) * ch + (z * 2 + c + 1)
        for mode, place in enumerate((by_y, by_z)):
            code = jnp.where(held, place.astype(F32) + rank * (2.0 * n), 0.0)
            picks[mode] = jnp.where(level == k, code, picks[mode])
            picks[mode] = jnp.where(level == 4 + k, gates[k:k + 1], picks[mode])
    info[0] = picks[0]
    info[1] = picks[1]
    pl.semaphore_wait(barrier, 4 * n - 3 + 2)

    pending = []

    def go(copy):
        copy.start()
        pending.append(copy)
        return copy

    psib = jnp.where(first, z, y)
    mine = pl.ds(pl.multiple_of(c * tok, tok), tok)
    mycol = pl.ds(pl.multiple_of(c * wh, wh), wh)
    hiscol = pl.ds(pl.multiple_of((1 - c) * wh, wh), wh)
    def first_step(a, way, h):
        k = 1 if way == 0 else -1
        if h == 0:
            to, at, cols = ring(k), p, mycol
        else:
            zz, yy = lax.rem(z + k + n, n), lax.rem(y + k + n, n)
            to = {"expert": jnp.where(first, (y * n + zz) * 2 + 1, (yy * n + z) * 2)}
            at, cols = psib, hiscol
        src = (x_ref, dy_ref)[a].at[:, cols]
        return remote(src, buf.at[a, at, mine], fs_s.at[way, a, h], fs_r.at[way, a, c], to)

    slots = go(remote(info.at[1 - c], infor, p0_s.at[2], p0_r.at[2], sib))
    for a in range(2):
        for way in range(2):
            for h in range(2):
                go(first_step(a, way, h))
    swap = [
        slots,
        go(remote(x_ref.at[:, hiscol], buf.at[0, psib, mine], p0_s.at[0], p0_r.at[0], sib)),
        go(remote(dy_ref.at[:, hiscol], buf.at[1, psib, mine], p0_s.at[1], p0_r.at[1], sib)),
    ]

    wcopies = []
    for k, dst in enumerate((wgu, wdn)):
        fetch[k].wait()
        src = dst.at[d]
        wcopies.append(go(remote(src, dst.at[d], w_s.at[0, 0, k], w_r.at[0, 0, k], {"dp": right})))
        wcopies.append(go(remote(src, dst.at[d], w_s.at[0, 1, k], w_r.at[0, 1, k], {"dp": left})))
    buf[0, p, mine] = x_ref[:, mycol]
    buf[1, p, mine] = dy_ref[:, mycol]
    fetch[2].wait()

    def ag(s, way, a):
        at = lax.rem(p - s + n, n) if way == 0 else lax.rem(p + s, n)
        ref = buf.at[a, at, pl.ds(way * tok, tok)] if s == half_n - 1 else buf.at[a, at]
        return remote(ref, ref, ag_s.at[way, s, a], ag_r.at[way, s, a], ring(1 if way == 0 else -1))

    copies = {}

    def gather(s):
        for a in range(2):
            for way in range(2):
                if s == 1:
                    at = lax.rem(p + n - 1 if way == 0 else p + 1, n)
                    for m in range(2):
                        ref = buf.at[a, at, pl.ds(m * tok, tok)]
                        pltpu.make_async_copy(ref, ref, fs_r.at[way, a, m]).wait()
                else:
                    copies[s - 1, way, a].wait_recv()
            for way in range(2):
                copies[s, way, a] = go(ag(s, way, a))

    swap[0].wait_recv()
    infob[p] = info[c] + infor[...]

    @pl.loop(1, n)
    def _(k):
        remote(infob.at[p], infob.at[p], in_s.at[k], in_r.at[p], ring(k)).start()

    gather(1)

    @pl.loop(1, n)
    def _(k):
        at = lax.rem(p + k, n)
        pltpu.make_async_copy(infob.at[at], infob.at[at], in_r.at[at]).wait()

    @pl.loop(0, n)
    def _(at):
        block = infob[at]
        rows = lax.broadcasted_iota(jnp.int32, (2 * n * ch, lanes), 0).astype(F32)
        picked = jnp.zeros((2 * n * ch, lanes), F32)
        scaled = jnp.zeros((2 * n * ch, lanes), F32)
        for k in range(4):
            hit = rows == (block[k:k + 1, :] - base)
            picked = jnp.where(hit, 1.0, picked)
            scaled = jnp.where(hit, block[4 + k:5 + k, :], scaled)
        cols = pl.ds(pl.multiple_of(at * lanes, lanes), lanes)
        sel[0, :, cols] = picked.astype(BF)
        sel[1, :, cols] = scaled.astype(BF)

    for s in range(2, half_n):
        gather(s)

    def dispatch(a):
        swap[1 + a].wait_recv()
        for way in range(2):
            copies[half_n - 1, way, a].wait_recv()

        @pl.loop(0, half_n)
        def _(g):
            places = (lax.rem(bm + g, n), lax.rem(bm + g + half_n, n))
            spans = [pl.ds(pl.multiple_of(b * (2 * ch), 2 * ch), 2 * ch) for b in places]
            lhs = jnp.concatenate([sel[a, span, :] for span in spans], axis=0)
            rows = dot(lhs, buf[a].reshape(n * lanes, wh)).astype(BF)
            for i, (b, span) in enumerate(zip(places, spans)):
                sb[a, span, :] = rows[i * 2 * ch:(i + 1) * 2 * ch]
                for cc in range(2):
                    src = sb.at[a, pl.ds(pl.multiple_of((b * 2 + cc) * ch, ch), ch)]
                    dst = xs.at[a, c, pl.ds(pl.multiple_of(bm * ch, ch), ch)]
                    own = jnp.logical_and(b == bm, c == cc)

                    @pl.when(own)
                    def _():
                        pltpu.make_async_copy(src, dst, a2_r.at[a, c, bm]).start()

                    @pl.when(jnp.logical_not(own))
                    def _():
                        remote(src, dst, a2_s.at[a, b * 2 + cc], a2_r.at[a, c, bm], other(b, cc)).start()

    def arrived(a):
        @pl.loop(0, n)
        def _(b):
            for h in range(2):
                ref = xs.at[a, h, pl.ds(pl.multiple_of(b * ch, ch), ch)]
                pltpu.make_async_copy(ref, ref, a2_r.at[a, h, b]).wait()

        xs[a, 1] = dot(perm[...], xs[a, 1]).astype(BF)

    dispatch(0)
    dispatch(1)
    halfb = blk // 2
    for copy in wcopies:
        copy.wait_recv()
    wc2 = []
    for k, dst in enumerate((wgu, wdn)):
        top, low = dst.at[left, pl.ds(0, halfb)], dst.at[right, pl.ds(halfb, halfb)]
        wc2.append(go(remote(top, top, w_s.at[1, 0, k], w_r.at[1, 0, k], {"dp": right})))
        wc2.append(go(remote(low, low, w_s.at[1, 1, k], w_r.at[1, 1, k], {"dp": left})))

    def part(t):
        per = wh // blk
        return t // per, pl.ds(pl.multiple_of(lax.rem(t, per) * blk, blk), blk)

    arrived(0)
    blocks = []
    for k in range(3):
        to = lax.rem(d + k + 1, dpn)
        h, cols = part(to)
        blocks.append(go(remote(xs.at[0, h, :, cols], xa.at[d], xb_s.at[k], xb_r.at[k], {"dp": to})))
    for copy in wc2:
        copy.wait_recv()
    wgu_h = [wgu[h * dpn // 2:(h + 1) * dpn // 2].reshape(wh, 2 * hid) for h in range(2)]
    wdn_h = [wdn[h * dpn // 2:(h + 1) * dpn // 2].reshape(wh, hid) for h in range(2)]
    pre_s[...] = dot(xs[0, 0], wgu_h[0]) + dot(xs[0, 1], wgu_h[1])
    arrived(1)
    gh = dot(xs[1, 0], wdn_h[0]) + dot(xs[1, 1], wdn_h[1])
    gate, up = pre_s[:, :hid], pre_s[:, hid:]
    sig = jax.nn.sigmoid(gate)
    act = gate * sig
    hidden = (act * up).astype(BF)
    hid_s[...] = hidden
    gp_s[:, :hid] = (gh * up * sig * (1.0 + gate * (1.0 - sig))).astype(BF)
    gp_s[:, hid:] = (gh * act).astype(BF)
    bulk = [go(remote(gp_s, gpa.at[d], gp_sem_s.at[0, way], gp_sem_r.at[0, way], {"dp": to}))
            for way, to in ((0, right), (1, left))]
    for h in range(2):
        rows = dot(gp_s[...], wgu_h[h], ((1,), (1,))).astype(BF)
        if h == 1:
            rows = dot(perm[...], rows).astype(BF)
        ret[h] = rows

        @pl.loop(0, n)
        def _(i):
            b = lax.rem(bm + i, n)
            src = ret.at[h, pl.ds(pl.multiple_of(b * ch, ch), ch)]
            q = (z if h == 0 else y) * 2 + c
            dst = back.at[pl.ds(pl.multiple_of(q * ch, ch), ch)]
            own = jnp.logical_and(c == h, b == bm)

            @pl.when(own)
            def _():
                pltpu.make_async_copy(src, dst, bk_r.at[q]).start()

            @pl.when(jnp.logical_not(own))
            def _():
                to = dev(y, b, 0) if h == 0 else dev(b, z, 1)
                remote(src, dst, bk_s.at[h, b], bk_r.at[q], to).start()

    def down_part(t):
        h, cols = part(t)
        return dot(xs[1, h, :, cols], hid_s[...], ((0,), (0,)))

    both = ((0, {"dp": right}, 0), (1, {"dp": left}, halfb))
    d0[...] = down_part(lax.rem(d + 2, dpn)).astype(BF)
    far_copies = [go(remote(d0.at[pl.ds(off, halfb)], r0.at[way], dp_s.at[0, way], dp_r.at[0, way], to))
                  for way, to, off in both]

    weight_grad = jnp.sum(hidden.astype(F32) * gh, axis=1, keepdims=True)
    ranks = weight_grad.reshape(n, cap, 2 * n, 1)
    lane = lax.broadcasted_iota(jnp.int32, (n, 2 * n, LANES), 2)
    packed = jnp.zeros((n, 2 * n, LANES), F32)
    for r in range(cap):
        packed = jnp.where(lane == r, ranks[:, r], packed)
    g_out[...] = packed.astype(BF)

    @pl.loop(0, n)
    def _(b):
        own = jnp.logical_and(first, b == bm)

        @pl.when(own)
        def _():
            pltpu.make_async_copy(g_out.at[b], g_in.at[z * 2 + c], gb_r.at[z * 2 + c]).start()

        @pl.when(jnp.logical_not(own))
        def _():
            remote(g_out.at[b], g_in.at[z * 2 + c], gb_s.at[b], gb_r.at[z * 2 + c], dev(y, b, 0)).start()

    here_h, here_cols = part(d)
    ddn_ref[...] = down_part(d)
    dgu_v[...] = dot(xs[0, here_h, :, here_cols], gp_s[...], ((0,), (0,)))
    half_rows = n * ch // 2
    for copy in bulk:
        copy.wait_recv()
    top, low = gpa.at[left, pl.ds(0, half_rows)], gpa.at[right, pl.ds(half_rows, half_rows)]
    rest = [go(remote(top, top, gp_sem_s.at[1, 0], gp_sem_r.at[1, 0], {"dp": right})),
            go(remote(low, low, gp_sem_s.at[1, 1], gp_sem_r.at[1, 1], {"dp": left}))]

    near = []
    for way, to, off in both:
        dn = down_part(right if way == 0 else left)
        far_copies[way].wait_recv()
        d1[way] = dn.astype(BF)
        here = slice(off, off + halfb)
        d1[way, here] = (dn[here] + r0[way].astype(F32)).astype(BF)
        near.append(go(remote(d1.at[way], r1.at[way], dp_s.at[1, way], dp_r.at[1, way], to)))
    def add_block(t):
        dgu_v[...] += dot(xa[t], gpa[t], ((0,), (0,)))

    @pl.loop(0, 2 * n)
    def _(q):
        ref = back.at[pl.ds(pl.multiple_of(q * ch, ch), ch)]
        pltpu.make_async_copy(ref, ref, bk_r.at[q]).wait()

    def share(t):
        cols = pl.ds(pl.multiple_of(t * lanes, lanes), lanes)
        return dot(sel[0, :, cols], back[...], ((0,), (0,)))

    pieces = 4
    piece = lanes // pieces

    def rows_of(m):
        return slice(m * piece, (m + 1) * piece)

    def rs(s, way, m):
        rows = pl.ds(m * piece, piece)
        k = 1 if way == 0 else -1
        if s < half_n - 1:
            return remote(rs_out.at[way, s, rows], rs_in.at[way, s, rows],
                          rs_s.at[way, s, m], rs_r.at[way, s, m], ring(k))
        at = lax.rem(p + k + n, n)
        owner = m * 2 // pieces
        to = {"expert": jnp.where(first, (at * n + z) * 2, (y * n + at) * 2) + owner}
        i = m % (pieces // 2)
        return remote(rs_out.at[way, s, rows], last_in.at[c, way, pl.ds(i * piece, piece)],
                      rs_s.at[way, s, m], last_r.at[c, way, i], to)

    def rs_runs(s, way, m):
        return s > 0 or m // (pieces // 2) == way

    whole = share(lax.rem(p + half_n, n)).astype(BF)
    rcopies = {}
    for m in range(pieces):
        for way in range(2):
            if rs_runs(0, way, m):
                rs_out[way, 0, rows_of(m)] = whole[rows_of(m)]
                rcopies[0, way, m] = go(rs(0, way, m))

    @pl.when(first)
    def _():
        @pl.loop(0, 2 * n)
        def _(q):
            pltpu.make_async_copy(g_in.at[q], g_in.at[q], gb_r.at[q]).wait()

        lane3 = lax.broadcasted_iota(jnp.int32, (2 * n, 2 * n, LANES), 2)
        packed_in = g_in[...].astype(F32)
        for r in range(cap):
            value = jnp.sum(jnp.where(lane3 == r, packed_in, 0.0), axis=2, keepdims=True)
            g_col[:, r] = jnp.broadcast_to(value, (2 * n, 2 * n, lanes))

        @pl.loop(0, n)
        def _(i):
            at = lax.rem(p + i, n)
            block = infob[at]
            rows = lax.broadcasted_iota(jnp.int32, (2 * n * ch, lanes), 0).astype(F32)
            column = g_col[...].reshape(2 * n * ch, lanes)
            tile = jnp.zeros((8, lanes), F32)
            for k in range(4):
                hit = rows == (block[k:k + 1, :] - base)
                found = jnp.sum(jnp.where(hit, column, 0.0), axis=0, keepdims=True)
                tile = jnp.where(level == k, found, tile)
            g_part[at] = tile

            @pl.when(i == 0)
            def _():
                pltpu.make_async_copy(g_part.at[at], g_all.at[p], gs_r.at[p]).start()

            @pl.when(i != 0)
            def _():
                remote(g_part.at[at], g_all.at[p], gs_s.at[at], gs_r.at[p], dev(at, z, 0)).start()

    def taken(s, way, m, held_part):
        if not rs_runs(s, way, m):
            return held_part
        rcopies[s, way, m].wait_recv()
        return held_part + rs_in[way, s, rows_of(m)].astype(F32)

    for s in range(1, half_n):
        shares = [share(lax.rem(p + half_n - s if way == 0 else p + half_n + s, n)) for way in range(2)]
        for m in range(pieces):
            for way in range(2):
                rs_out[way, s, rows_of(m)] = taken(s - 1, way, m, shares[way][rows_of(m)]).astype(BF)
                rcopies[s, way, m] = go(rs(s, way, m))
        if s == 1:
            for copy in blocks:
                copy.wait_recv()
            add_block(left)
        if s == 2:
            add_block(right)
    fin[...] = share(p).astype(BF)
    his = pl.ds(pl.multiple_of((1 - c) * tok, tok), tok)
    swapped = go(remote(fin.at[his], finr, f_s, f_r, sib))
    swapped.wait_recv()

    def finish(h, way, i):
        there = last_in.at[h, way, pl.ds(i * piece, piece)]
        pltpu.make_async_copy(there, there, last_r.at[h, way, i]).wait()
        return last_in[h, way, i * piece:(i + 1) * piece].astype(F32)

    for i in range(pieces // 2):
        span = slice(i * piece, (i + 1) * piece)
        for h, cols, begun in ((c, mycol, fin[pl.ds(pl.multiple_of(c * tok + i * piece, piece), piece), :]),
                               (1 - c, hiscol, finr[span])):
            value = begun.astype(F32)
            for way in range(2):
                value = value + finish(h, way, i)
            gt_ref[span, cols] = value.astype(BF)

    @pl.when(first)
    def _():
        g_sum = jnp.zeros((8, lanes), F32)
        for src in range(n):
            pltpu.make_async_copy(g_all.at[src], g_all.at[src], gs_r.at[src]).wait()
            g_sum = g_sum + g_all[src]
        g_fin[...] = g_sum
        remote(g_fin, g_part.at[0], gf_s, gf_r, sib).start()

    for copy in rest:
        copy.wait_recv()
    if half_n < 3:
        add_block(right)
    add_block(lax.rem(d + 2, dpn))
    leaving = pltpu.make_async_copy(dgu_v, dgu_ref, out_s)
    leaving.start()
    for copy in near:
        copy.wait_recv()
    ddn_ref[...] += r1[0].astype(F32) + r1[1].astype(F32)

    @pl.when(first)
    def _():
        pltpu.make_async_copy(g_fin, g_fin, gf_s).wait()

        @pl.loop(1, n)
        def _(i):
            at = lax.rem(p + i, n)
            pltpu.make_async_copy(g_part.at[at], g_part.at[at], gs_s.at[at]).wait()

    @pl.when(c == 1)
    def _():
        pltpu.make_async_copy(g_fin, g_fin, gf_r).wait()
        g_fin[...] = g_part[0]

    quotient = jnp.where(held, g_fin[0:4], 0.0) / jnp.where(held, info[0, 4:8], 1.0)
    gr_ref[...] = dot(quotient.astype(BF), spread, ((1,), (1,))).astype(BF)

    leaving.wait()
    for copy in pending:
        copy.wait_send()

    @pl.loop(1, n)
    def _(k):
        pltpu.make_async_copy(infob.at[p], infob.at[p], in_s.at[k]).wait()

    @pl.loop(0, n)
    def _(b):
        for a in range(2):
            for cc in range(2):
                @pl.when(jnp.logical_not(jnp.logical_and(b == bm, c == cc)))
                def _():
                    ref = sb.at[a, pl.ds(pl.multiple_of((b * 2 + cc) * ch, ch), ch)]
                    pltpu.make_async_copy(ref, ref, a2_s.at[a, b * 2 + cc]).wait()
        for h in range(2):
            @pl.when(jnp.logical_not(jnp.logical_and(c == h, b == bm)))
            def _():
                ref = ret.at[h, pl.ds(pl.multiple_of(b * ch, ch), ch)]
                pltpu.make_async_copy(ref, ref, bk_s.at[h, b]).wait()
                if h == 0:
                    pltpu.make_async_copy(g_out.at[b], g_out.at[b], gb_s.at[b]).wait()


def hand_over(*refs):
    count = len(refs) // 4
    ins, outs, rooms = refs[:count], refs[count:2 * count], refs[2 * count:3 * count]
    sems = refs[3 * count:]
    moves = []
    for src, dst, room, (come, leave) in zip(ins, outs, rooms, [(s.at[0], s.at[1]) for s in sems]):
        rows = src.shape[0]
        step = rows // 4 if rows >= 64 else rows
        for i in range(0, rows, step):
            part = pl.ds(i, step)
            moves.append((pltpu.make_async_copy(src.at[part], room.at[part], come.at[i // step]),
                          pltpu.make_async_copy(room.at[part], dst.at[part], leave.at[i // step])))
    for come, _ in moves:
        come.start()
    for come, leave in moves:
        come.wait()
        leave.start()
    for _, leave in moves:
        leave.wait()


def on_device(n, dpn, tokens, grad_out, route_expert, route_weight, gate_up_weight, down_weight):
    tok, width = tokens.shape
    top = route_expert.shape[1]
    wh = width // 2
    blk, hid = down_weight.shape[1:]
    experts = 2 * n * n
    cap = min(tok, (tok * top + experts - 1) // experts + 1)
    ch = 2 * n * cap
    lanes = 2 * tok
    at = np.arange(n * ch)
    hop = (at % (2 * n)) // 2 * ch + (at % ch) // (2 * n) * (2 * n) + at // ch * 2 + at % 2
    perm = np.zeros((n * ch, n * ch), np.float32)
    perm[at, hop] = 1.0
    perm = jnp.asarray(perm, BF)

    vm = pl.BlockSpec(memory_space=pltpu.VMEM)
    half_n = n // 2
    dma = pltpu.SemaphoreType.DMA
    all_rows = 2 * n * ch
    wx = wh
    scratch = [
        pltpu.VMEM((2, n, lanes, wh), BF),
        pltpu.VMEM((2, 8, lanes), F32),
        pltpu.VMEM((n, 8, lanes), F32),
        pltpu.VMEM((8, lanes), F32),
        pltpu.VMEM((2, all_rows, n * lanes), BF),
        pltpu.VMEM((2, all_rows, wh), BF),
        pltpu.VMEM((2, 2, n * ch, wh), BF),
        pltpu.VMEM((dpn, blk, 2 * hid), BF),
        pltpu.VMEM((dpn, blk, hid), BF),
        pltpu.VMEM((n * ch, 2 * hid), F32),
        pltpu.VMEM((n * ch, 2 * hid), BF),
        pltpu.VMEM((n * ch, hid), BF),
        pltpu.VMEM((2, n * ch, wx), BF),
        pltpu.VMEM((all_rows, wx), BF),
        pltpu.VMEM((2, half_n, lanes, wx), BF),
        pltpu.VMEM((2, half_n, lanes, wx), BF),
        pltpu.VMEM((lanes, wx), BF),
        pltpu.VMEM((tok, wx), BF),
        pltpu.VMEM((blk, hid), BF),
        pltpu.VMEM((2, blk, hid), BF),
        pltpu.VMEM((2, blk // 2, hid), BF),
        pltpu.VMEM((2, blk, hid), BF),
        pltpu.VMEM((dpn, n * ch, blk), BF),
        pltpu.VMEM((dpn, n * ch, 2 * hid), BF),
        pltpu.VMEM((n, 2 * n, LANES), BF),
        pltpu.VMEM((2 * n, 2 * n, LANES), BF),
        pltpu.VMEM((2 * n, cap, 2 * n, lanes), F32),
        pltpu.VMEM((n, 8, lanes), F32),
        pltpu.VMEM((n, 8, lanes), F32),
        pltpu.VMEM((8, lanes), F32),
        dma((3,)), dma((3,)),
        dma((2, half_n, 2)), dma((2, half_n, 2)),
        dma((n,)), dma((n,)),
        dma((2, 2 * n)), dma((2, 2, n)),
        dma((2, 2, 2)), dma((2, 2, 2)),
        dma((2, n)), dma((2 * n,)),
        dma((2, half_n, 4)), dma((2, half_n, 4)),
        dma, dma,
        dma((2, 2)), dma((2, 2)),
        dma((n,)), dma((2 * n,)),
        dma((n,)), dma((n,)),
        dma, dma,
        dma((3,)), dma((3,)),
        dma((2, 2)), dma((2, 2)),
        pltpu.VMEM((n * ch, n * ch), BF),
        dma((3,)),
        pltpu.VMEM((2, 2, tok, wx), BF),
        dma((2, 2, 2)),
        pltpu.VMEM((blk, 2 * hid), F32),
        dma,
        dma((2, 2, 2)), dma((2, 2, 2)),
    ]
    grad_tokens, grad_w, grad_gu, grad_dn = pl.pallas_call(
        functools.partial(kernel, n, cap, dpn),
        out_shape=(
            jax.ShapeDtypeStruct((tok, width), BF),
            jax.ShapeDtypeStruct((top, tok), BF),
            jax.ShapeDtypeStruct((blk, 2 * hid), F32),
            jax.ShapeDtypeStruct((blk, hid), F32),
        ),
        in_specs=[vm] * 4 + [pl.BlockSpec(memory_space=pl.ANY)] * 3,
        out_specs=(vm, vm, pl.BlockSpec(memory_space=pl.ANY), vm),
        scratch_shapes=scratch,
        compiler_params=pltpu.CompilerParams(
            collective_id=0, has_side_effects=True, vmem_limit_bytes=60 * 1024 * 1024),
    )(tokens, grad_out, route_expert.T, route_weight.T, perm, gate_up_weight[0], down_weight[0])
    grad_route = grad_w.T
    results = (grad_tokens, grad_gu, grad_dn)
    hbm = pl.BlockSpec(memory_space=pl.ANY)
    grad_tokens, grad_gu, grad_dn = pl.pallas_call(
        hand_over,
        out_shape=tuple(jax.ShapeDtypeStruct(r.shape, r.dtype) for r in results),
        in_specs=[hbm] * 3,
        out_specs=(hbm,) * 3,
        scratch_shapes=[pltpu.VMEM(r.shape, r.dtype) for r in results] + [dma((2, 4))] * 3,
        compiler_params=pltpu.CompilerParams(vmem_limit_bytes=60 * 1024 * 1024),
    )(*results)
    return grad_tokens, grad_route, grad_gu[None], grad_dn[None]


def solution(mesh):
    n = math.isqrt(mesh.shape["expert"] // 2)
    return jax.shard_map(
        functools.partial(on_device, n, mesh.shape["dp"]),
        mesh=mesh,
        in_specs=(
            P(("expert", "dp"), None),
            P(("expert", "dp"), None),
            P(("expert", "dp"), None),
            P(("expert", "dp"), None),
            P("expert", "dp", None),
            P("expert", "dp", None),
        ),
        out_specs=(
            P(("expert", "dp"), None),
            P(("expert", "dp"), None),
            P("expert", "dp", None),
            P("expert", "dp", None),
        ),
        check_vma=False,
    )
```
